32 devices in a mesh: groups: 2 (over y), queue: 4 (over z), heads: 2 (over x), seq: 2 (over core).
Axes of the slice: x: 2, y: 2, z: 4, core: 2. Of those that a mesh axis runs over, the one named last changes fastest.
Arguments:
- latent: bfloat16 [32, 128, 5120], P(('groups', 'queue', 'seq'), None, 'heads'), parts along dimension 0, may hold values from -6 to 6
- projections: bfloat16 [3, 32, 128, 3072], P(None, ('groups', 'queue', 'seq'), None, 'heads'), parts along dimension 1, may hold values from -32 to 32
- frame_times: int32 [32], P(('groups', 'queue', 'seq')), parts along dimension 0, may hold values from 1 to 112, as said below
- levels: int32 [8], P(('groups', 'queue')), parts along dimension 0, may hold values from 0 to 49
- gates: bfloat16 [50, 5120], P(None, 'heads'), may hold values from -6 to 6
- out_weight: bfloat16 [3072, 5120], P('heads', 'queue'), may hold values from -0.109375 to 0.109375
- incoming_latent: bfloat16 [4, 128, 5120], P('groups', None, 'heads'), parts along dimension 0, may hold values from -6 to 6
- incoming_proj: bfloat16 [4, 3, 128, 3072], P('groups', None, None, 'heads'), parts along dimension 0, may hold values from -32 to 32
- incoming_times: int32 [4], P('groups'), parts along dimension 0, may hold values from 115 to 118, as said below
Outputs:
- advanced_latent: bfloat16 [32, 128, 5120], P(('groups', 'queue', 'seq'), None, 'heads'), parts along dimension 0
The draws below stay inside these ranges and needn't reach their ends.
There are 2 independent parts, one for each index of `groups`. The reference program is written for one: setup_inputs(seed, part) draws one part's arguments, and reference() takes and returns one part's arrays. A program takes and returns all parts, laid end to end along the dimension named above; an argument that names none is the same for every part. Nothing has to cross between parts.
Inputs may be any that keep to these rules, and one draw needn't show every extreme that they name: `frame_times`: rise strictly from frame to frame. `incoming_times`: rise strictly and all exceed the last of frame_times.
All inputs are finite; a program needn't handle non-finite values.
Results may differ from the reference program's by a relative error of at most 0.011.
Values may be sent and summed in bfloat16 or wider, within the bound.
No kernel may reach another device: no remote copies, remote signals or barrier semaphores. Data moves between devices by JAX's collectives and lax.ppermute only.
A program may use at most 128 MiB of HBM per device.

```python
import math
import jax
import jax.numpy as jnp
from jax import lax

D = 5120
HEADS = 24
HD = 128
FT = 128
FRAMES = 4
ADV = 2
STEPS = 50
NF = 16
QUEUE_LEN = 4
C = 3072
N_QUEUE = 4
N_HEADS = 2


def scaled(drawn_base):
    return jnp.stack([2.0 * drawn_base[0], drawn_base[1], drawn_base[2]]).astype(jnp.bfloat16)


def clock(key):
    gaps_all = jax.random.randint(jax.random.fold_in(key, 8), (NF + ADV,), 1, 4)
    top_frame = 3 * NF + 64
    frame_gaps = gaps_all[:NF]
    frame_after = jnp.cumsum(frame_gaps[::-1])[::-1] - frame_gaps
    frame_part = top_frame - frame_after
    enter_gaps = gaps_all[NF:]
    enter_after = jnp.cumsum(enter_gaps[::-1])[::-1] - enter_gaps
    enter_part = top_frame + 3 * ADV - enter_after
    return jnp.concatenate([frame_part, enter_part])


def draw_projections(key, part):
    key = jax.random.fold_in(key, 1)
    return scaled(jax.random.truncated_normal(key, -4.0, 4.0, (3, NF, FT, HEADS * HD), jnp.float32))


def draw_incoming_proj(key, part):
    key = jax.random.fold_in(key, 2)
    result = scaled(jax.random.truncated_normal(key, -4.0, 4.0, (3, ADV, FT, HEADS * HD), jnp.float32))
    return jnp.transpose(result, (1, 0, 2, 3))


def draw_frame_times(key, part):
    shared = clock(key)
    return shared[:NF].astype(jnp.int32)


def draw_incoming_times(key, part):
    shared = clock(key)
    return shared[NF:].astype(jnp.int32)


def plant(values, key, low, largest):
    shape = values.shape
    spot = [jax.random.randint(jax.random.fold_in(key, axis), (), 0, shape[axis]) for axis in range(len(shape))]
    values = values.at[tuple(spot)].set(low)
    longest = shape.index(max(shape))
    spot[longest] = (spot[longest] + 1) % shape[longest]
    return values.at[tuple(spot)].set(largest)


def block_levels(key, shape, shards, least, largest):
    level, own = 1.0, jax.random.fold_in(key, 6)
    for position, shards_of in shards:
        steps = jnp.exp(jax.random.uniform(jax.random.fold_in(own, position), (shards_of,), jnp.float32, least / len(shards), largest / len(shards)))
        level = level * jnp.repeat(steps, shape[position] // shards_of).reshape([-1 if axis == position else 1 for axis in range(len(shape))])
    return level


def scatter_about(key, dims, scale, bound, cuts=(), held_as=jnp.bfloat16):
    values = scale * jax.random.normal(key, dims, jnp.float32)
    if cuts:
        values = values * block_levels(key, dims, cuts, -0.22, 0.18)
    return jnp.clip(values, -bound, bound).astype(held_as)


def setup_inputs(seed: int = 0, part: int = 0) -> dict:
    arg_keys = jax.random.split(jax.random.key(seed), 10)
    own_keys = jax.random.split(jax.random.fold_in(arg_keys[9], part), 10)
    return {
        "latent": scatter_about(own_keys[0], (NF, FT, D), 1.0, 6.0, ((0, 8), (2, 2))),
        "projections": draw_projections(jax.random.fold_in(jax.random.fold_in(arg_keys[9], part), 71), part),
        "frame_times": draw_frame_times(jax.random.fold_in(jax.random.fold_in(arg_keys[9], part), 71), part),
        "levels": plant(jax.random.randint(own_keys[3], (QUEUE_LEN,), 0, STEPS), jax.random.fold_in(own_keys[3], 1), 0, STEPS - 1).astype(jnp.int32),
        "gates": scatter_about(arg_keys[4], (STEPS, D), 1.5, 6.0, ((1, 2),)),
        "out_weight": scatter_about(arg_keys[5], (C, D), C ** -0.5, 0.109375, ((0, 2), (1, 4))),
        "incoming_latent": scatter_about(own_keys[6], (ADV, FT, D), 1.0, 6.0, ((2, 2),)),
        "incoming_proj": draw_incoming_proj(jax.random.fold_in(jax.random.fold_in(arg_keys[9], part), 71), part),
        "incoming_times": draw_incoming_times(jax.random.fold_in(jax.random.fold_in(arg_keys[9], part), 71), part),
    }


def rotate_pairs(block_in, times_in, head_dim):
    frames, tokens, channels = block_in.shape
    half_dim = head_dim // 2
    pair_index = jnp.arange(half_dim, dtype=jnp.float32)
    frequency = jnp.power(jnp.float32(10000.0), -pair_index / half_dim)
    angles = times_in.astype(jnp.float32)[:, None] * frequency[None, :]
    cosine = jnp.cos(angles)[:, None, None, :]
    sine_term = jnp.sin(angles)[:, None, None, :]
    head_view = block_in.astype(jnp.float32).reshape(frames, tokens, channels // head_dim, head_dim)
    first_half = head_view[..., :half_dim]
    second_half = head_view[..., half_dim:]
    turned = jnp.concatenate([first_half * cosine - second_half * sine_term, second_half * cosine + first_half * sine_term], axis=-1)
    return turned.reshape(frames, tokens, channels).astype(jnp.bfloat16)

def rotate_all(projection, times_in, head_dim):
    return jnp.stack([rotate_pairs(projection[0], times_in, head_dim), rotate_pairs(projection[1], times_in, head_dim), projection[2]])

def attend(queries, key_rows, value_rows, usable, head_dim):
    row_count, channels = queries.shape
    head_count = channels // head_dim
    query_heads = queries.astype(jnp.float32).reshape(row_count, head_count, head_dim)
    key_heads = key_rows.astype(jnp.float32).reshape(-1, head_count, head_dim)
    value_heads = value_rows.astype(jnp.float32).reshape(-1, head_count, head_dim)
    scores = jnp.einsum('rhd,khd->hrk', query_heads, key_heads) * (1.0 / math.sqrt(head_dim))
    scores = jnp.where(usable[None, None, :], scores, -1e+30)
    row_top = lax.optimization_barrier(jnp.max(scores, axis=-1, keepdims=True))
    weights = jnp.exp(scores - row_top)
    weights = (weights / lax.optimization_barrier(jnp.sum(weights, axis=-1, keepdims=True))).astype(jnp.bfloat16)
    mixture = jnp.einsum('hrk,khd->rhd', weights.astype(jnp.float32), value_heads)
    return mixture.reshape(row_count, channels).astype(jnp.bfloat16)

def reference(latent, projections, frame_times, levels, gates, out_weight, incoming_latent, incoming_proj, incoming_times):
    carried = rotate_all(projections, frame_times, HD)
    fresh_proj = rotate_all(jnp.transpose(incoming_proj, (1, 0, 2, 3)), incoming_times, HD)
    group_cols = HEADS // N_HEADS * HD
    gate_rows = jnp.repeat(gates.astype(jnp.float32)[levels], FRAMES, axis=0)
    for advance in range(ADV):
        latent = jnp.concatenate([latent[1:], incoming_latent[advance][None]], axis=0)
        carried = jnp.concatenate([carried[:, 1:], fresh_proj[:, advance:advance + 1]], axis=1)
        padded = jnp.pad(carried[1:], ((0, 0), (1, 1), (0, 0), (0, 0)))

        def one_window(window_id):
            first_frame = (window_id * FRAMES).astype(jnp.int32)
            queries = lax.dynamic_slice_in_dim(carried[0], first_frame, FRAMES, 0).reshape(FRAMES * FT, -1)
            nearby = lax.dynamic_slice_in_dim(padded, first_frame, FRAMES + 2, 1)
            key_rows = nearby[0].reshape(-1, nearby.shape[-1])
            value_rows = nearby[1].reshape(-1, nearby.shape[-1])
            frame_ok = jnp.ones((FRAMES + 2,), dtype=bool).at[0].set(window_id > 0).at[FRAMES + 1].set(window_id < N_QUEUE - 1)
            usable = jnp.repeat(frame_ok, FT)
            return attend(queries, key_rows, value_rows, usable, HD)
        mixture = lax.map(one_window, jnp.arange(N_QUEUE, dtype=jnp.int32)).reshape(NF * FT, -1)
        update = jnp.zeros((NF * FT, D), jnp.float32)
        for head_group in range(N_HEADS):
            lower = head_group * group_cols
            product = jnp.dot(mixture[:, lower:lower + group_cols], out_weight[lower:lower + group_cols], preferred_element_type=jnp.float32)
            rounded = lax.optimization_barrier(product.astype(jnp.bfloat16))
            update = update + rounded.astype(jnp.float32)
        latent = (latent.astype(jnp.float32) + gate_rows[:, None, :] * update.reshape(NF, FT, D)).astype(jnp.bfloat16)
    return latent
```

```python
import functools
import math

import jax
import jax.numpy as jnp
from jax import lax
from jax.experimental import pallas as pl
from jax.experimental.pallas import tpu as pltpu
from jax.sharding import PartitionSpec as P

HD = 128
BF16 = jnp.bfloat16
F32 = jnp.float32
VMEM_LIMIT = 48 * 1024 * 1024


def params(*semantics):
    return pltpu.CompilerParams(
        dimension_semantics=semantics, vmem_limit_bytes=VMEM_LIMIT
    )


def rotation_tables(times):
    half = HD // 2
    pair_index = jnp.arange(half, dtype=F32)
    frequency = jnp.power(F32(10000.0), -pair_index / half)
    angles = times.astype(F32)[:, None] * frequency[None, :]
    cosine, sine = jnp.cos(angles), jnp.sin(angles)
    return (
        jnp.concatenate([cosine, cosine], axis=1),
        jnp.concatenate([-sine, sine], axis=1),
    )


def rotate_kernel(core_ref, cos_ref, sin_ref, own_ref, new_ref, q_ref, kv_ref, side_ref, nq_ref, nkv_ref):
    frames = own_ref.shape[1]
    heads = own_ref.shape[-1] // HD
    first_core = core_ref[0] == 0

    def turn(block, row):
        block = block.astype(F32)
        out = block * cos_ref[row : row + 1, :] + pltpu.roll(block, HD // 2, 1) * sin_ref[row : row + 1, :]
        return out.astype(BF16)

    for head in range(heads):
        at = slice(head * HD, (head + 1) * HD)
        for frame in range(frames):
            query = turn(own_ref[0, frame, :, at], frame)
            q_ref[frame, :, at] = query
            kv_ref[0, frame, :, at] = turn(own_ref[1, frame, :, at], frame)
            kv_ref[1, frame, :, at] = own_ref[2, frame, :, at]
            nq_ref[frame, :, at] = turn(new_ref[frame, 0, :, at], frames + frame)
            nkv_ref[0, frame, :, at] = turn(new_ref[frame, 1, :, at], frames + frame)
            nkv_ref[1, frame, :, at] = new_ref[frame, 2, :, at]

    @pl.when(first_core)
    def _():
        side_ref[...] = q_ref[...]

    @pl.when(jnp.logical_not(first_core))
    def _():
        side_ref[0] = kv_ref[0, 0]
        side_ref[1] = kv_ref[1, 0]


def rotate_all(core, cos, sin, own, new):
    _, frames, tokens, channels = own.shape
    wide = min(channels, 3 * HD)
    steps = channels // wide
    three = pl.BlockSpec((frames, tokens, wide), lambda i, c: (0, 0, i))
    four = pl.BlockSpec((2, frames, tokens, wide), lambda i, c: (0, 0, 0, i))
    table = pl.BlockSpec(cos.shape, lambda i, c: (0, 0))
    sq = jax.ShapeDtypeStruct((frames, tokens, channels), BF16)
    skv = jax.ShapeDtypeStruct((2, frames, tokens, channels), BF16)
    return pl.pallas_call(
        rotate_kernel,
        grid_spec=pltpu.PrefetchScalarGridSpec(
            num_scalar_prefetch=1,
            grid=(steps,),
            in_specs=[
                table,
                table,
                pl.BlockSpec((3, frames, tokens, wide), lambda i, c: (0, 0, 0, i)),
                pl.BlockSpec((frames, 3, tokens, wide), lambda i, c: (0, 0, 0, i)),
            ],
            out_specs=[three, four, three, three, four],
        ),
        out_shape=[sq, skv, sq, sq, skv],
        compiler_params=params("arbitrary"),
        cost_estimate=pl.CostEstimate(flops=10 * own.size, bytes_accessed=10 * own.size, transcendentals=0),
        name="rotate",
    )(core, cos, sin, own, new)


def attend_kernel(
    where_ref, peer_q, far_q, new_q, own_kv, peer_kv, far_kv, new_kv, far6_kv, send_ref, keep_ref, key_s, value_s
):
    tokens = peer_q.shape[1]
    core, first, last = where_ref[0], where_ref[1] == 1, where_ref[2] == 1
    second_core = core == 1
    for side, scratch in ((0, key_s), (1, value_s)):
        for frame in range(2):
            own, peer = own_kv[side, frame], peer_kv[side, frame]
            scratch[pl.ds(frame * tokens, tokens), :] = jnp.where(second_core, peer, own)
            scratch[pl.ds((2 + frame) * tokens, tokens), :] = jnp.where(second_core, own, peer)
            scratch[pl.ds((4 + frame) * tokens, tokens), :] = jnp.where(
                last, new_kv[side, frame], far_kv[side, frame]
            )
        scratch[pl.ds(6 * tokens, tokens), :] = far6_kv[side]
    q4 = jnp.where(last, new_q[0], far_q[0])
    q5 = jnp.where(last, new_q[1], far_q[1])
    qa = jnp.where(second_core, q4, peer_q[0])
    qb = peer_q[1]
    qc = jnp.where(second_core, q5, peer_q[1])
    factor = math.log2(math.e) / math.sqrt(HD)
    keys = key_s[...]
    scores = lax.dot_general(
        jnp.concatenate([qa, qb, qc], axis=0), keys, (((1,), (1,)), ((), ())), preferred_element_type=F32
    )

    def mix(rows, low):
        part = [rows[:, (low + i) * tokens : (low + i + 1) * tokens] for i in range(6)]
        part[0] = jnp.where(first, -1e30, part[0])
        part[5] = jnp.where(last, -1e30, part[5])
        rows = jnp.concatenate(part, axis=1)
        top = jnp.max(rows, axis=1, keepdims=True)
        weights = jnp.exp2((rows - top) * factor)
        total = jnp.sum(weights, axis=1, keepdims=True)
        out = jnp.dot(
            weights.astype(BF16), value_s[pl.ds(low * tokens, 6 * tokens), :], preferred_element_type=F32
        )
        return (out * (1.0 / total)).astype(BF16)

    early = mix(scores[: 2 * tokens], 0)
    late = mix(jnp.concatenate([scores[:tokens], scores[2 * tokens :]], axis=0), 1)
    keep_ref[0] = early[:tokens]
    send_ref[...] = early[tokens:]
    keep_ref[1] = late[:tokens]
    keep_ref[2] = late[tokens:]


def attend_all(where, peer_q, far_q, new_q, own_kv, peer_kv, far_kv, new_kv, far6_kv):
    _, tokens, channels = peer_q.shape
    heads = channels // HD
    three = pl.BlockSpec((2, tokens, HD), lambda i, c: (0, 0, i))
    four = pl.BlockSpec((2, 2, tokens, HD), lambda i, c: (0, 0, 0, i))
    return pl.pallas_call(
        attend_kernel,
        grid_spec=pltpu.PrefetchScalarGridSpec(
            num_scalar_prefetch=1,
            grid=(heads,),
            in_specs=[three, three, three, four, four, four, four, three],
            out_specs=[
                pl.BlockSpec((tokens, HD), lambda i, c: (0, i)),
                pl.BlockSpec((3, tokens, HD), lambda i, c: (0, 0, i)),
            ],
            scratch_shapes=[pltpu.VMEM((7 * tokens, HD), BF16), pltpu.VMEM((7 * tokens, HD), BF16)],
        ),
        out_shape=[
            jax.ShapeDtypeStruct((tokens, channels), BF16),
            jax.ShapeDtypeStruct((3, tokens, channels), BF16),
        ],
        compiler_params=params("arbitrary"),
        cost_estimate=pl.CostEstimate(
            flops=heads * 4 * 4 * 6 * tokens * tokens * HD,
            bytes_accessed=26 * tokens * channels * 2,
            transcendentals=heads * 4 * 6 * tokens * tokens,
        ),
        name="attend",
    )(where, peer_q, far_q, new_q, own_kv, peer_kv, far_kv, new_kv, far6_kv)


def project_kernel(order_ref, *refs):
    count = (len(refs) - 2) // 2
    mixes, pieces, gate_ref, out_ref = refs[:count], refs[count : 2 * count], refs[-2], refs[-1]
    total = None
    for mix, piece in zip(mixes, pieces):
        product = jnp.dot(mix[...], piece[...], preferred_element_type=F32)
        total = product if total is None else total + product
    frames, tokens = 2, out_ref.shape[0] // 2
    for frame in range(frames):
        a, b = frame * tokens, (frames + frame) * tokens
        out_ref[a : a + tokens, :] = (
            total[a : a + tokens] * gate_ref[frame : frame + 1, :]
            + total[b : b + tokens] * gate_ref[frames + frame : frames + frame + 1, :]
        ).astype(BF16)


def project(order, mix, pieces, whole, gates, wide=256):
    count = len(pieces)
    rows, channels = mix.shape
    depth = channels // count
    columns = pieces[0].shape[1]
    if depth % HD or columns % wide:
        total = 0.0
        for i, piece in enumerate(pieces):
            piece = lax.slice_in_dim(piece, i * depth, (i + 1) * depth, axis=0) if whole else piece
            part = lax.dynamic_slice_in_dim(mix, order[i] * depth, depth, axis=1)
            total = total + jnp.dot(part, piece, preferred_element_type=F32)
        total = total.reshape(4, rows // 4, columns) * gates[:, None, :]
        return (total[:2] + total[2:]).reshape(rows // 2, columns).astype(BF16)

    def mix_at(p):
        return pl.BlockSpec((rows, depth), lambda i, c: (0, c[p]))

    def piece_at(p):
        return pl.BlockSpec((depth, wide), lambda i, c: (p if whole else 0, i))

    return pl.pallas_call(
        project_kernel,
        grid_spec=pltpu.PrefetchScalarGridSpec(
            num_scalar_prefetch=1,
            grid=(columns // wide,),
            in_specs=[mix_at(p) for p in range(count)]
            + [piece_at(p) for p in range(count)]
            + [pl.BlockSpec((4, wide), lambda i, c: (0, i))],
            out_specs=pl.BlockSpec((rows // 2, wide), lambda i, c: (0, i)),
        ),
        out_shape=jax.ShapeDtypeStruct((rows // 2, columns), BF16),
        compiler_params=params("arbitrary"),
        cost_estimate=pl.CostEstimate(
            flops=2 * rows * channels * columns,
            bytes_accessed=2 * (rows * channels + channels * columns + rows * columns // 2),
            transcendentals=0,
        ),
        name="project",
    )(order, *([mix] * count), *pieces, gates)


def arrivals(count):
    table = []
    for k in range(1, count):
        row = []
        for q in range(count):
            ahead, behind = count - 1 - q, q
            if q < count // 2:
                row.append(("down", k) if k <= ahead else ("up", k - ahead))
            else:
                row.append(("up", k) if k <= behind else ("down", k - behind))
        table.append(row)
    return table


def pick(place, row, held):
    value = None
    for source in sorted(set(row)):
        here = jnp.array([r == source for r in row])[place]
        value = held[source] if value is None else jnp.where(here, held[source], value)
    return value


def local(
    latent,
    projections,
    frame_times,
    levels,
    gates,
    out_weight,
    incoming_latent,
    incoming_proj,
    incoming_times,
):
    place, count = lax.axis_index("queue"), lax.axis_size("queue")
    core, cores = lax.axis_index("seq"), lax.axis_size("seq")
    side, sides = lax.axis_index("heads"), lax.axis_size("heads")
    group, groups = lax.axis_index("groups"), lax.axis_size("groups")
    first, last = place == 0, place == count - 1
    frames, tokens, features = latent.shape
    assert cores == 2 and frames == 2 and groups == 2 and count % sides == 0

    depth = out_weight.shape[0] // 4
    mine = group * 2 + core
    quarter = lax.dynamic_slice_in_dim(out_weight, mine * depth, depth, axis=0)
    held = {}
    up = down = quarter
    for hop in range(1, count):
        up = lax.ppermute(up, "queue", [(i, i + 1) for i in range(hop - 1, count - 1)])
        down = lax.ppermute(down, "queue", [(i, i - 1) for i in range(1, count - hop + 1)])
        held["up", hop], held["down", hop] = up, down

    cos, sin = rotation_tables(jnp.concatenate([frame_times, incoming_times]))
    where = jnp.stack([core, first.astype(jnp.int32), last.astype(jnp.int32)])
    own_q, own_kv, side_out, new_q, new_kv = rotate_all(where, cos, sin, projections, incoming_proj)
    swap = [(0, 1), (1, 0)]
    pair = ("queue", "seq")
    far_kv = lax.ppermute(own_kv, pair, [(2 * i + 2, 2 * i) for i in range(count - 1)])
    side_in = lax.ppermute(
        side_out, pair, [(2 * i + 2 + s, 2 * i + 1 - s) for i in range(count - 1) for s in range(2)]
    )
    peer_q = lax.ppermute(own_q, "seq", swap)
    peer_kv = lax.ppermute(own_kv, "seq", swap)
    far_kv_1 = lax.ppermute(far_kv, "seq", [(0, 1)])
    far6_1 = lax.ppermute(side_in, "seq", [(0, 1)])
    far_kv = jnp.where(core == 0, far_kv, far_kv_1)
    far6 = jnp.where(core == 0, side_in, far6_1)

    send, keep = attend_all(where, peer_q, side_in, new_q, own_kv, peer_kv, far_kv, new_kv, far6)
    came = lax.ppermute(send, pair, [(2 * i + 3, 2 * i + 1) for i in range(count - 1)])
    mix = jnp.concatenate(
        [keep[0], jnp.where(core == 0, send, came), keep[1], keep[2]], axis=0
    )

    next_level = lax.ppermute(levels, "queue", [(i + 1, i) for i in range(count - 1)])
    chosen = jnp.concatenate([levels, next_level])
    one_hot = (jnp.arange(gates.shape[0], dtype=jnp.int32)[None, :] == chosen[:, None]).astype(BF16)
    rows = jnp.dot(one_hot, gates, preferred_element_type=F32).astype(BF16)
    rows = lax.all_gather(rows, "heads", axis=1, tiled=True).astype(F32)
    crossing = jnp.where(last, 0.0, rows[1:2])
    gate_rows = jnp.concatenate(
        [rows[:1], jnp.where(core == 0, rows[:1], crossing), rows[:1], rows[:1]], axis=0
    )

    moved = lax.ppermute(latent, pair, [(i + 1, i) for i in range(2 * count - 1)])
    moved = jnp.where(jnp.logical_and(last, core == 1), incoming_latent, moved)
    moved = moved.reshape(frames * tokens, features)

    columns = out_weight.shape[1]
    per_side = count // sides
    table = arrivals(count)
    block_of = [list(range(count))]
    for row in table:
        block_of.append([q + hops if way == "down" else q - hops for q, (way, hops) in enumerate(row)])
    flat = ("queue", "heads")
    deltas, others, blocks = [], [], []
    for k in range(count):
        block = jnp.array(block_of[k], jnp.int32)[place]
        gate = lax.dynamic_slice_in_dim(gate_rows, block * columns, columns, axis=1)
        if k == 0:
            pieces, order = [out_weight] * 4, jnp.arange(4, dtype=jnp.int32)
        else:
            a = pick(place, table[k - 1], held)
            b = lax.ppermute(a, "groups", swap)
            c = lax.ppermute(a, "seq", swap)
            d = lax.ppermute(b, "seq", swap)
            pieces = [a, b, c, d]
            order = jnp.stack([mine, mine ^ 2, mine ^ 1, mine ^ 3]).astype(jnp.int32)
        delta = project(order, mix, pieces, k == 0, gate)
        deltas.append(delta)
        blocks.append(block)
        if sides == 2:
            pairs = [
                (q * 2 + 1 - block_of[k][q] // per_side, q * 2 + block_of[k][q] // per_side)
                for q in range(count)
            ]
            others.append(lax.ppermute(delta, flat, pairs))

    if sides == 2:
        parts = []
        for b in range(per_side):
            wanted = side * per_side + b
            total = moved[:, b * columns : (b + 1) * columns].astype(F32)
            change = jnp.zeros_like(total)
            for delta, other, block in zip(deltas, others, blocks):
                change = jnp.where(block == wanted, delta.astype(F32) + other.astype(F32), change)
            parts.append(total + change)
        total = jnp.concatenate(parts, axis=1)
    else:
        change = jnp.zeros((frames * tokens, columns * count), BF16)
        for delta, block in zip(deltas, blocks):
            change = lax.dynamic_update_slice_in_dim(change, delta, block * columns, axis=1)
        change = lax.psum_scatter(change, "heads", scatter_dimension=1, tiled=True)
        total = moved.astype(F32) + change.astype(F32)
    return total.astype(BF16).reshape(frames, tokens, features)


def solution(mesh):
    return jax.shard_map(
        local,
        mesh=mesh,
        in_specs=(
            P(("groups", "queue", "seq"), None, "heads"),
            P(None, ("groups", "queue", "seq"), None, "heads"),
            P(("groups", "queue", "seq")),
            P(("groups", "queue")),
            P(None, "heads"),
            P("heads", "queue"),
            P("groups", None, "heads"),
            P("groups", None, None, "heads"),
            P("groups"),
        ),
        out_specs=P(("groups", "queue", "seq"), None, "heads"),
        check_vma=False,
    )
```

```python
import functools
import math

import jax
import jax.numpy as jnp
from jax import lax
from jax.experimental import pallas as pl
from jax.experimental.pallas import tpu as pltpu
from jax.sharding import PartitionSpec as P

HD = 128
BF16 = jnp.bfloat16
F32 = jnp.float32
VMEM_LIMIT = 16 * 1024 * 1024


COST = pl.CostEstimate(flops=1000, bytes_accessed=1000, transcendentals=0)


def params(*semantics):
    return pltpu.CompilerParams(dimension_semantics=semantics or None, vmem_limit_bytes=VMEM_LIMIT)


def rotation_tables(times):
    half = HD // 2
    pair_index = jnp.arange(half, dtype=F32)
    frequency = jnp.power(F32(10000.0), -pair_index / half)
    angles = times.astype(F32)[:, None] * frequency[None, :]
    cosine, sine = jnp.cos(angles), jnp.sin(angles)
    return (
        jnp.concatenate([cosine, cosine], axis=1),
        jnp.concatenate([-sine, sine], axis=1),
    )


def rotate_kernel(core_ref, cos_ref, sin_ref, own_ref, new_ref, q_ref, kv_ref, side_ref, nq_ref, nkv_ref):
    frames = own_ref.shape[1]
    heads = own_ref.shape[-1] // HD
    first_core = core_ref[0] == 0

    def turn(block, row):
        block = block.astype(F32)
        out = block * cos_ref[row : row + 1, :] + pltpu.roll(block, HD // 2, 1) * sin_ref[row : row + 1, :]
        return out.astype(BF16)

    for head in range(heads):
        at = slice(head * HD, (head + 1) * HD)
        for frame in range(frames):
            query = turn(own_ref[0, frame, :, at], frame)
            q_ref[frame, :, at] = query
            kv_ref[0, frame, :, at] = turn(own_ref[1, frame, :, at], frame)
            kv_ref[1, frame, :, at] = own_ref[2, frame, :, at]
            nq_ref[frame, :, at] = turn(new_ref[frame, 0, :, at], frames + frame)
            nkv_ref[0, frame, :, at] = turn(new_ref[frame, 1, :, at], frames + frame)
            nkv_ref[1, frame, :, at] = new_ref[frame, 2, :, at]

    @pl.when(first_core)
    def _():
        side_ref[...] = q_ref[...]

    @pl.when(jnp.logical_not(first_core))
    def _():
        side_ref[0] = kv_ref[0, 0]
        side_ref[1] = kv_ref[1, 0]


def rotate_all(core, cos, sin, own, new):
    _, frames, tokens, channels = own.shape
    wide = min(channels, 3 * HD)
    steps = channels // wide
    three = pl.BlockSpec((frames, tokens, wide), lambda i, c: (0, 0, i))
    four = pl.BlockSpec((2, frames, tokens, wide), lambda i, c: (0, 0, 0, i))
    table = pl.BlockSpec(cos.shape, lambda i, c: (0, 0))
    sq = jax.ShapeDtypeStruct((frames, tokens, channels), BF16)
    skv = jax.ShapeDtypeStruct((2, frames, tokens, channels), BF16)
    return pl.pallas_call(
        rotate_kernel,
        grid_spec=pltpu.PrefetchScalarGridSpec(
            num_scalar_prefetch=1,
            grid=(steps,),
            in_specs=[
                table,
                table,
                pl.BlockSpec((3, frames, tokens, wide), lambda i, c: (0, 0, 0, i)),
                pl.BlockSpec((frames, 3, tokens, wide), lambda i, c: (0, 0, 0, i)),
            ],
            out_specs=[three, four, three, three, four],
        ),
        out_shape=[sq, skv, sq, sq, skv],
        compiler_params=params("arbitrary"),
        cost_estimate=COST,
        name="rotate",
    )(core, cos, sin, own, new)


def attend_kernel(
    where_ref, peer_q, far_q, new_q, own_kv, peer_kv, far_kv, far_kv_1, new_kv, far6_kv_1, send_ref, keep_ref
):
    tokens = peer_q.shape[1]
    heads = peer_q.shape[-1] // HD
    core, first, last = where_ref[0], where_ref[1] == 1, where_ref[2] == 1
    second_core = core == 1
    factor = math.log2(math.e) / math.sqrt(HD)

    def one(at):
        def frames_of(side):
            own = [own_kv[side, frame, :, at] for frame in range(2)]
            peer = [peer_kv[side, frame, :, at] for frame in range(2)]
            rows = [jnp.where(second_core, p, o) for o, p in zip(own, peer)]
            rows += [jnp.where(second_core, o, p) for o, p in zip(own, peer)]
            for frame in range(2):
                far = jnp.where(second_core, far_kv_1[side, frame, :, at], far_kv[side, frame, :, at])
                rows.append(jnp.where(last, new_kv[side, frame, :, at], far))
            return rows + [jnp.where(second_core, far6_kv_1[side, :, at], far_q[side, :, at])]

        keys, values = frames_of(0), frames_of(1)

        def mix(query, low):
            rows = lax.dot_general(
                query,
                jnp.concatenate(keys[low : low + 6], axis=0),
                (((1,), (1,)), ((), ())),
                preferred_element_type=F32,
            )
            part = [rows[:, i * tokens : (i + 1) * tokens] for i in range(6)]
            part[0] = jnp.where(first, -1e30, part[0])
            part[5] = jnp.where(last, -1e30, part[5])
            rows = jnp.concatenate(part, axis=1)
            top = jnp.max(rows, axis=1, keepdims=True)
            weights = jnp.exp2((rows - top) * factor)
            total = jnp.sum(weights, axis=1, keepdims=True)
            out = jnp.dot(
                weights.astype(BF16),
                jnp.concatenate(values[low : low + 6], axis=0),
                preferred_element_type=F32,
            )
            return (out * (1.0 / total)).astype(BF16)

        q4 = jnp.where(last, new_q[0, :, at], far_q[0, :, at])
        q5 = jnp.where(last, new_q[1, :, at], far_q[1, :, at])
        qa = jnp.where(second_core, q4, peer_q[0, :, at])
        qc = jnp.where(second_core, q5, peer_q[1, :, at])
        early = mix(jnp.concatenate([qa, peer_q[1, :, at]], axis=0), 0)
        late = mix(jnp.concatenate([qa, qc], axis=0), 1)
        keep_ref[0, :, at] = early[:tokens]
        send_ref[:, at] = early[tokens:]
        keep_ref[1, :, at] = late[:tokens]
        keep_ref[2, :, at] = late[tokens:]

    group = 4 if heads % 4 == 0 else 1

    @pl.loop(0, heads // group)
    def _(step):
        for head in range(group):
            one(pl.ds(pl.multiple_of((step * group + head) * HD, HD), HD))


def attend(where, *operands):
    _, tokens, channels = operands[0].shape
    return pl.pallas_call(
        attend_kernel,
        in_specs=[pl.BlockSpec(memory_space=pltpu.SMEM)] + [pl.BlockSpec(memory_space=pltpu.VMEM)] * len(operands),
        out_specs=[pl.BlockSpec(memory_space=pltpu.VMEM)] * 2,
        out_shape=[
            jax.ShapeDtypeStruct((tokens, channels), BF16),
            jax.ShapeDtypeStruct((3, tokens, channels), BF16),
        ],
        compiler_params=params(),
        cost_estimate=COST,
        name="attend",
    )(where, *operands)


def project_kernel(half, place_ref, mix_ref, gate_ref, *refs):
    pieces, out_ref = refs[:-1], refs[-1]
    group, core, gate_at = place_ref[0], place_ref[1], place_ref[2]
    channels = mix_ref.shape[1]
    tokens = mix_ref.shape[0] // 8
    depth = channels // 2
    if len(pieces) == 1:
        widths = [256] * (half // 256) + [half % 256] * (half % 256 > 0)
    else:
        widths = [piece.shape[1] for piece in pieces[::2]]
    low = 0
    for i, wide in enumerate(widths):
        if len(pieces) == 1:
            at = pl.ds(pl.multiple_of(core * half + low, HD), wide)
            total = jnp.dot(mix_ref[...], pieces[0][:, at], preferred_element_type=F32)
        else:
            near = mix_ref[:, pl.ds(pl.multiple_of(group * depth, HD), depth)]
            far = mix_ref[:, pl.ds(pl.multiple_of((1 - group) * depth, HD), depth)]
            total = jnp.dot(near, pieces[2 * i][...], preferred_element_type=F32)
            total = total + jnp.dot(far, pieces[2 * i + 1][...], preferred_element_type=F32)
        at = pl.ds(pl.multiple_of(gate_at + low, HD), wide)
        row = gate_ref[0:1, at]
        parts = [total[n * tokens : (n + 1) * tokens] for n in range(8)]
        for who in range(2):
            crossing = gate_ref[1 + who : 2 + who, at]
            p = parts[4 * who : 4 * who + 4]
            base = 2 * who * tokens
            out_ref[base : base + tokens, low : low + wide] = ((p[0] + p[2]) * row).astype(BF16)
            out_ref[base + tokens : base + 2 * tokens, low : low + wide] = (p[1] * crossing + p[3] * row).astype(BF16)
        low += wide


def project(group, core, half, gate_at, mix, pieces, gates):
    rows, channels = mix.shape
    columns = half if len(pieces) == 1 else sum(piece.shape[1] for piece in pieces[::2])
    depth = channels // 2
    if depth % HD or half % HD:
        if len(pieces) == 1:
            weights = lax.dynamic_slice_in_dim(pieces[0], core * half, half, axis=1)
        else:
            weights = [
                jnp.where(group == 0, jnp.concatenate([own, other]), jnp.concatenate([other, own]))
                for own, other in zip(pieces[::2], pieces[1::2])
            ]
            weights = jnp.concatenate(weights, axis=1)
        total = jnp.dot(mix, weights, preferred_element_type=F32).reshape(2, 4, rows // 8, columns)
        gates = lax.dynamic_slice_in_dim(gates, gate_at, columns, axis=1)
        even = (total[:, 0] + total[:, 2]) * gates[0]
        odd = total[:, 1] * gates[1:, None, :] + total[:, 3] * gates[0]
        return jnp.stack([even, odd], axis=1).reshape(rows // 2, columns).astype(BF16)

    place = jnp.stack([group, core, gate_at]).astype(jnp.int32)
    return pl.pallas_call(
        functools.partial(project_kernel, half),
        in_specs=[pl.BlockSpec(memory_space=pltpu.SMEM)]
        + [pl.BlockSpec(memory_space=pltpu.VMEM)] * (2 + len(pieces)),
        out_specs=pl.BlockSpec(memory_space=pltpu.VMEM),
        out_shape=jax.ShapeDtypeStruct((rows // 2, columns), BF16),
        compiler_params=params(),
        cost_estimate=COST,
        name="project",
    )(place, mix, gates, *pieces)


def arrivals(count):
    table = []
    for k in range(1, count):
        row = []
        for q in range(count):
            ahead, behind = count - 1 - q, q
            if q < count // 2:
                row.append(("down", k) if k <= ahead else ("up", k - ahead))
            else:
                row.append(("up", k) if k <= behind else ("down", k - behind))
        table.append(row)
    return table


def pick(place, row, held):
    value = None
    for source in sorted(set(row)):
        here = functools.reduce(jnp.logical_or, [place == q for q, r in enumerate(row) if r == source])
        value = held(source) if value is None else jnp.where(here, held(source), value)
    return value


def look_up(place, row):
    return sum(jnp.where(place == q, value, 0) for q, value in enumerate(row))


def after(value, *done):
    return lax.optimization_barrier((value, done))[0]


def local(
    latent,
    projections,
    frame_times,
    levels,
    gates,
    out_weight,
    incoming_latent,
    incoming_proj,
    incoming_times,
):
    place, count = lax.axis_index("queue"), lax.axis_size("queue")
    core, cores = lax.axis_index("seq"), lax.axis_size("seq")
    side, sides = lax.axis_index("heads"), lax.axis_size("heads")
    group, groups = lax.axis_index("groups"), lax.axis_size("groups")
    first, last = place == 0, place == count - 1
    frames, tokens, features = latent.shape
    assert cores == 2 and frames == 2 and groups == 2 and count % sides == 0
    columns = out_weight.shape[1]
    half = columns // 2
    swap = [(0, 1), (1, 0)]
    pair = ("queue", "seq")
    table = arrivals(count)
    block_of = [list(range(count))]
    for row in table:
        block_of.append([q + hops if way == "down" else q - hops for q, (way, hops) in enumerate(row)])

    next_level = lax.ppermute(levels, "queue", [(i + 1, i) for i in range(count - 1)])
    depth = out_weight.shape[0] // 2
    cuts = [0, half]
    if half % HD == 0 and half > HD:
        cuts = [0, (half // HD + 1) // 2 * HD, half]
    chunks = list(zip(cuts[:-1], cuts[1:]))
    origin = lax.dynamic_slice(out_weight, (group * depth, core * half), (depth, half))
    whole = [(0, half)]
    held = {}

    def send_weights(name, block, low, hops, ends):
        for way, part, sign in (("up", block[0], 1), ("down", block[1], -1)):
            pairs = [(i, i + hops) for i in range(count - hops) if i >= ends]
            if sign < 0:
                pairs = [(count - 1 - i, count - 1 - j) for i, j in pairs]
            held[way, name, low] = lax.ppermute(part, "queue", pairs)

    gathered = {}

    def spread(k, low, high, *done):
        sources = {key: held[key + (0,)] for key in table[k - 1]}
        if done:
            sources = after(sources, *done)
        own = pick(place, table[k - 1], lambda key: sources[key][:, low:high])
        gathered[k, low] = (own, lax.ppermute(own, "groups", swap))
        return own

    send_weights(1, (origin, origin), 0, 1, 0)
    if count > 2:
        send_weights(2, (held["up", 1, 0], held["down", 1, 0]), 0, 1, 1)

    spread(1, 0, half)

    cos, sin = rotation_tables(jnp.concatenate([frame_times, incoming_times]))
    where = jnp.stack([core, first.astype(jnp.int32), last.astype(jnp.int32)])
    own_q, own_kv, side_out, new_q, new_kv = rotate_all(where, cos, sin, projections, incoming_proj)
    peer_q = lax.ppermute(own_q, "seq", swap)
    peer_kv = lax.ppermute(own_kv, "seq", swap)
    side_in = lax.ppermute(
        side_out, pair, [(2 * i + 2 + s, 2 * i + 1 - s) for i in range(count - 1) for s in range(2)]
    )
    far_kv = lax.ppermute(own_kv, pair, [(2 * i + 2, 2 * i) for i in range(count - 1)])
    far6_1 = lax.ppermute(after(side_in, gathered[1, 0][0]), "seq", [(0, 1)])
    far_kv = after(far_kv, peer_q, peer_kv, gathered[1, 0][1], held["up", 2, 0], held["down", 2, 0])
    far_kv_1 = lax.ppermute(far_kv, "seq", [(0, 1)])
    inputs = (peer_q, side_in, new_q, own_kv, peer_kv, far_kv, far_kv_1, new_kv, far6_1)

    send, keep = attend(where, *inputs)
    came = lax.ppermute(send, pair, [(2 * i + 3, 2 * i + 1) for i in range(count - 1)])
    for hop in range(3, count):
        send_weights(hop, (held["up", hop - 1, 0], held["down", hop - 1, 0]), 0, 1, hop - 1)
        came = after(came, spread(hop - 1, 0, half))
    k = count - 1
    for low, high in chunks:
        came = after(came, spread(k, low, high, keep))
    peer_keep = lax.ppermute(keep, "seq", swap)
    second = jnp.where(core == 0, send, came)
    peer_second = lax.ppermute(second, "seq", swap)
    mix = jnp.concatenate(
        [keep[0], second, keep[1], keep[2], peer_keep[0], peer_second, peer_keep[1], peer_keep[2]], axis=0
    )

    moved = lax.ppermute(after(latent, second), pair, [(i + 1, i) for i in range(2 * count - 1)])
    moved = jnp.where(jnp.logical_and(last, core == 1), incoming_latent, moved)
    moved = moved.reshape(frames * tokens, features)

    chosen = jnp.concatenate([levels, after(next_level, far_kv)])
    one_hot = (jnp.arange(gates.shape[0], dtype=jnp.int32)[None, :] == chosen[:, None]).astype(BF16)
    rows = jnp.dot(one_hot, gates, preferred_element_type=F32).astype(BF16)
    if sides == 2:
        other = lax.ppermute(rows, "heads", swap)
        rows = jnp.concatenate(
            [jnp.where(side == 0, rows, other), jnp.where(side == 0, other, rows)], axis=1
        )
    else:
        rows = lax.all_gather(rows, "heads", axis=1, tiled=True)
    rows = rows.astype(F32)
    crossing = jnp.where(last, 0.0, rows[1:2])
    gate_rows = jnp.concatenate(
        [rows[:1], jnp.where(core == 0, rows[:1], crossing), jnp.where(core == 0, crossing, rows[:1])], axis=0
    )

    per_side = count // sides
    flat = ("queue", "heads")

    def summed(k, pieces, low, *done):
        block = look_up(place, block_of[k])
        rows = after(mix, *done) if done else mix
        delta = project(group, core, half, block * columns + core * half + low, rows, pieces, gate_rows)
        if sides != 2:
            return block, delta, None
        pairs = [
            (q * 2 + 1 - block_of[k][q] // per_side, q * 2 + block_of[k][q] // per_side) for q in range(count)
        ]
        return block, delta, lax.ppermute(delta, flat, pairs)

    results = [summed(0, [out_weight], 0)]
    for n in range(1, k):
        done = [gathered[k, low][1] for low, _ in chunks[n - 1 : n]]
        results.append(summed(n, gathered[n, 0], 0, *done))
    late = []
    for n, (low, high) in enumerate(chunks):
        own, other = gathered[k, low]
        other = after(other, *[part for part in results[0][1:] + results[min(n + 1, k - 1)][1:2] if part is not None])
        late.append((low, summed(k, [own, other], low)))
    if sides != 2:
        results += [result for _, result in late]
        change = jnp.zeros((2 * frames * tokens, count * half), BF16)
        for n, (block, delta, _) in enumerate(results):
            low = late[n - count + 1][0] if n >= count - 1 else 0
            change = lax.dynamic_update_slice_in_dim(change, delta, block * half + low, axis=1)
        early = lax.psum_scatter(change, "heads", scatter_dimension=1, tiled=True)
        late = []
    else:
        early = []
        for b in range(per_side):
            total = 0.0
            for block, delta, other in results:
                change = delta.astype(F32) + other.astype(F32)
                total = total + jnp.where(block == side * per_side + b, change, 0.0)
            early.append(total)
        early = jnp.concatenate(early, axis=1).astype(BF16)

    mine = frames * tokens
    early_back = lax.ppermute(early[mine:], "seq", swap)
    tail = []
    for low, (block, delta, other) in late:
        total = (delta.astype(F32) + other.astype(F32)).astype(BF16)
        tail.append((low, low + delta.shape[1], block, total[:mine], lax.ppermute(total[mine:], "seq", swap)))

    parts = []
    for b in range(per_side):
        for who in range(2):
            for low, high in chunks:
                at = b * half + low
                change = jnp.where(core == who, early[:mine, at : at + high - low], early_back[:, at : at + high - low])
                change = change.astype(F32)
                for start, _, block, own, back in tail:
                    if start == low:
                        last_part = jnp.where(core == who, own, back).astype(F32)
                        change = change + jnp.where(block == side * per_side + b, last_part, 0.0)
                at = b * columns + who * half + low
                parts.append((moved[:, at : at + high - low].astype(F32) + change).astype(BF16))
    return jnp.concatenate(parts, axis=1).reshape(frames, tokens, features)


def solution(mesh):
    return jax.shard_map(
        local,
        mesh=mesh,
        in_specs=(
            P(("groups", "queue", "seq"), None, "heads"),
            P(None, ("groups", "queue", "seq"), None, "heads"),
            P(("groups", "queue", "seq")),
            P(("groups", "queue")),
            P(None, "heads"),
            P("heads", "queue"),
            P("groups", None, "heads"),
            P("groups", None, None, "heads"),
            P("groups"),
        ),
        out_specs=P(("groups", "queue", "seq"), None, "heads"),
        check_vma=False,
    )
```

```python
import functools
import math

import jax
import jax.numpy as jnp
from jax import lax
from jax.experimental import pallas as pl
from jax.experimental.pallas import tpu as pltpu
from jax.sharding import PartitionSpec as P

HD = 128
BF16 = jnp.bfloat16
F32 = jnp.float32
SPARE = 16
VMEM_LIMIT = 16 * 1024 * 1024


COST = pl.CostEstimate(flops=1000, bytes_accessed=1000, transcendentals=0)


def params(*semantics):
    return pltpu.CompilerParams(dimension_semantics=semantics or None, vmem_limit_bytes=VMEM_LIMIT)


def rotation_tables(times):
    half = HD // 2
    pair_index = jnp.arange(half, dtype=F32)
    frequency = jnp.power(F32(10000.0), -pair_index / half)
    angles = times.astype(F32)[:, None] * frequency[None, :]
    cosine, sine = jnp.cos(angles), jnp.sin(angles)
    return (
        jnp.concatenate([cosine, cosine], axis=1),
        jnp.concatenate([-sine, sine], axis=1),
    )


def rotate_kernel(core_ref, cos_ref, sin_ref, own_ref, new_ref, mine_ref, peer_ref, peer_v_ref, fresh_ref):
    _, frames, _, channels = own_ref.shape
    share = mine_ref.shape[-1]

    def turn(block, row):
        block = block.astype(F32)
        out = block * cos_ref[row : row + 1, :] + pltpu.roll(block, HD // 2, 1) * sin_ref[row : row + 1, :]
        return out.astype(BF16)

    for head in range(share // HD):
        to = slice(head * HD, (head + 1) * HD)
        for target, core in ((mine_ref, core_ref[0]), (peer_ref, 1 - core_ref[0])):
            start = core * share if share < channels else 0
            at = pl.ds(pl.multiple_of(start + head * HD, HD), HD)
            for frame in range(frames):
                target[0, frame, :, to] = turn(own_ref[0, frame, :, at], frame)
                target[1, frame, :, to] = turn(own_ref[1, frame, :, at], frame)
                if target is mine_ref:
                    target[2, frame, :, to] = own_ref[2, frame, :, at]
                else:
                    peer_v_ref[frame, :, to] = own_ref[2, frame, :, at]
        start = core_ref[0] * share if share < channels else 0
        at = pl.ds(pl.multiple_of(start + head * HD, HD), HD)
        for frame in range(frames):
            fresh_ref[0, frame, :, to] = turn(new_ref[frame, 0, :, at], frames + frame)
            fresh_ref[1, frame, :, to] = turn(new_ref[frame, 1, :, at], frames + frame)
            fresh_ref[2, frame, :, to] = new_ref[frame, 2, :, at]

def rotate_all(where, cos, sin, own, new):
    _, frames, tokens, channels = own.shape
    share = channels // 2 if channels % (2 * HD) == 0 else channels
    full = jax.ShapeDtypeStruct((3, frames, tokens, share), BF16)
    return pl.pallas_call(
        rotate_kernel,
        in_specs=[pl.BlockSpec(memory_space=pltpu.SMEM)] + [pl.BlockSpec(memory_space=pltpu.VMEM)] * 4,
        out_specs=[pl.BlockSpec(memory_space=pltpu.VMEM)] * 4,
        out_shape=[
            full,
            jax.ShapeDtypeStruct((2, frames, tokens, share), BF16),
            jax.ShapeDtypeStruct((frames, tokens, share), BF16),
            full,
        ],
        compiler_params=params(),
        cost_estimate=COST,
        name="rotate",
    )(where, cos, sin, own, new)


def bundle_kernel(where_ref, mine, got, got_v, out_ref):
    theirs = got.at[0], got.at[1], got_v
    tokens = mine.shape[2]
    second_core = where_ref[0] == 1
    for kind in range(3):
        for frame in range(2):
            at = (2 * kind + frame) * tokens
            out_ref[at : at + tokens, :] = jnp.where(second_core, theirs[kind][frame], mine[kind, frame])
    for kind in (1, 2):
        at = (5 + kind) * tokens
        out_ref[at : at + tokens, :] = jnp.where(second_core, mine[kind, 0], theirs[kind][0])
    level = jnp.full((SPARE, out_ref.shape[1]), where_ref[3].astype(F32))
    out_ref[8 * tokens :, :] = level.astype(BF16)


def bundle(where, mine, got, got_v):
    _, _, tokens, share = mine.shape
    return pl.pallas_call(
        bundle_kernel,
        in_specs=[pl.BlockSpec(memory_space=pltpu.SMEM)] + [pl.BlockSpec(memory_space=pltpu.VMEM)] * 3,
        out_specs=pl.BlockSpec(memory_space=pltpu.VMEM),
        out_shape=jax.ShapeDtypeStruct((8 * tokens + SPARE, share), BF16),
        compiler_params=params(),
        cost_estimate=COST,
        name="bundle",
    )(where, mine, got, got_v)


def attend_kernel(where_ref, mine, got, got_v, fresh, far_ref, send_ref, keep_ref):
    theirs = got.at[0], got.at[1], got_v
    tokens = mine.shape[2]
    heads = mine.shape[-1] // HD
    core, first, last = where_ref[0], where_ref[1] == 1, where_ref[2] == 1
    second_core = core == 1
    factor = math.log2(math.e) / math.sqrt(HD)

    def one(at):
        def frames_of(kind):
            own = [mine[kind, frame, :, at] for frame in range(2)]
            peer = [theirs[kind][frame, :, at] for frame in range(2)]
            rows = [jnp.where(second_core, p, o) for o, p in zip(own, peer)]
            rows += [jnp.where(second_core, o, p) for o, p in zip(own, peer)]
            for frame in range(2):
                far = far_ref[(2 * kind + frame) * tokens : (2 * kind + frame + 1) * tokens, at]
                rows.append(jnp.where(last, fresh[kind, frame, :, at], far))
            if kind:
                rows.append(far_ref[(5 + kind) * tokens : (6 + kind) * tokens, at])
            return rows

        queries, keys, values = frames_of(0), frames_of(1), frames_of(2)

        def mix(query, low):
            rows = lax.dot_general(
                jnp.concatenate(query, axis=0),
                jnp.concatenate(keys[low : low + 6], axis=0),
                (((1,), (1,)), ((), ())),
                preferred_element_type=F32,
            )
            part = [rows[:, i * tokens : (i + 1) * tokens] for i in range(6)]
            part[0] = jnp.where(first, -1e30, part[0])
            part[5] = jnp.where(last, -1e30, part[5])
            rows = jnp.concatenate(part, axis=1)
            top = jnp.max(rows, axis=1, keepdims=True)
            weights = jnp.exp2((rows - top) * factor)
            total = jnp.sum(weights, axis=1, keepdims=True)
            out = jnp.dot(
                weights.astype(BF16),
                jnp.concatenate(values[low : low + 6], axis=0),
                preferred_element_type=F32,
            )
            return (out * (1.0 / total)).astype(BF16)

        early = mix(queries[1:5], 0)
        send_ref[:, at] = early[:tokens]
        keep_ref[: 3 * tokens, at] = early[tokens:]
        keep_ref[3 * tokens :, at] = mix(queries[2:6], 1)

    group = 3 if heads % 3 == 0 else 1

    @pl.loop(0, heads // group)
    def _(step):
        for head in range(group):
            one(pl.ds(pl.multiple_of((step * group + head) * HD, HD), HD))


def attend(where, *operands):
    _, _, tokens, share = operands[0].shape
    return pl.pallas_call(
        attend_kernel,
        in_specs=[pl.BlockSpec(memory_space=pltpu.SMEM)] + [pl.BlockSpec(memory_space=pltpu.VMEM)] * len(operands),
        out_specs=[pl.BlockSpec(memory_space=pltpu.VMEM)] * 2,
        out_shape=[
            jax.ShapeDtypeStruct((tokens, share), BF16),
            jax.ShapeDtypeStruct((7 * tokens, share), BF16),
        ],
        compiler_params=params(),
        cost_estimate=COST,
        name="attend",
    )(where, *operands)


def project_kernel(half, place_ref, keep_ref, came_ref, peer_keep_ref, peer_came_ref, gate_ref, *refs):
    pieces, out_ref = refs[:-1], refs[-1]
    group, core, gate_at = place_ref[0], place_ref[1], place_ref[2]
    tokens, depth = came_ref.shape
    own = jnp.concatenate([keep_ref[...], came_ref[...]], axis=0)
    peer = jnp.concatenate([peer_keep_ref[...], peer_came_ref[...]], axis=0)
    if len(pieces) == 1:
        widths = [256] * (half // 256) + [half % 256] * (half % 256 > 0)
    else:
        widths = [piece.shape[1] for piece in pieces[::2]]
    low = 0
    for i, wide in enumerate(widths):
        if len(pieces) == 1:
            at = pl.ds(pl.multiple_of(core * half + low, HD), wide)
            near = pieces[0][pl.ds(pl.multiple_of(core * depth, HD), depth), at]
            far = pieces[0][pl.ds(pl.multiple_of((1 - core) * depth, HD), depth), at]
        else:
            here, there = pieces[2 * i][...], pieces[2 * i + 1][...]
            near = jnp.where(group == core, here, there)
            far = jnp.where(group == core, there, here)
        total = jnp.dot(own, near, preferred_element_type=F32)
        total = total + jnp.dot(peer, far, preferred_element_type=F32)
        at = pl.ds(pl.multiple_of(gate_at + low, HD), wide)
        row, crossing = gate_ref[0:1, at], gate_ref[1:2, at]
        order = (0, 1, 2, 7, 3, 4, 5, 6)
        parts = [total[n * tokens : (n + 1) * tokens] for n in order]
        for who in range(2):
            base = jnp.where(core == who, 0, 2 * tokens)
            for frame in range(2):
                n = 2 * who + frame
                gate = crossing if n == 3 else row
                result = (parts[n] * gate + parts[4 + n] * row).astype(BF16)
                out_ref[pl.ds(pl.multiple_of(base + frame * tokens, tokens), tokens), low : low + wide] = result
        low += wide


def project(group, core, half, gate_at, mix, pieces, gates):
    keep, came, peer_keep, peer_came = mix
    tokens, share = came.shape
    columns = half if len(pieces) == 1 else sum(piece.shape[1] for piece in pieces[::2])
    if 2 * share != pieces[0].shape[0] * (1 if len(pieces) == 1 else 2) or share % HD or half % HD:
        if len(pieces) == 1:
            weights = lax.dynamic_slice_in_dim(pieces[0], core * half, half, axis=1)
        else:
            weights = [
                jnp.where(group == 0, jnp.concatenate([own, other]), jnp.concatenate([other, own]))
                for own, other in zip(pieces[::2], pieces[1::2])
            ]
            weights = jnp.concatenate(weights, axis=1)
        rows = jnp.concatenate([keep, came], axis=0)
        if 2 * share == weights.shape[0]:
            peer = jnp.concatenate([peer_keep, peer_came], axis=0)
            rows = jnp.where(
                core == 0, jnp.concatenate([rows, peer], axis=1), jnp.concatenate([peer, rows], axis=1)
            )
        total = jnp.dot(rows, weights, preferred_element_type=F32).reshape(8, tokens, columns)
        gates = lax.dynamic_slice_in_dim(gates, gate_at, columns, axis=1)
        first = jnp.stack([total[0], total[1], total[2], total[7]])
        scale = jnp.stack([gates[0], gates[0], gates[0], gates[1]])[:, None, :]
        total = (first * scale + total[3:7] * gates[0]).reshape(2, 2 * tokens, columns)
        total = jnp.where(core == 0, total, total[::-1])
        return total.reshape(4 * tokens, columns).astype(BF16)

    place = jnp.stack([group, core, gate_at]).astype(jnp.int32)
    return pl.pallas_call(
        functools.partial(project_kernel, half),
        in_specs=[pl.BlockSpec(memory_space=pltpu.SMEM)]
        + [pl.BlockSpec(memory_space=pltpu.VMEM)] * (5 + len(pieces)),
        out_specs=pl.BlockSpec(memory_space=pltpu.VMEM),
        out_shape=jax.ShapeDtypeStruct((4 * tokens, columns), BF16),
        compiler_params=params(),
        cost_estimate=COST,
        name="project",
    )(place, *mix, gates, *pieces)


def arrivals(count):
    table = []
    for k in range(1, count):
        row = []
        for q in range(count):
            ahead, behind = count - 1 - q, q
            if q < count // 2:
                row.append(("down", k) if k <= ahead else ("up", k - ahead))
            else:
                row.append(("up", k) if k <= behind else ("down", k - behind))
        table.append(row)
    return table


def pick(place, row, held):
    value = None
    for source in sorted(set(row)):
        here = functools.reduce(jnp.logical_or, [place == q for q, r in enumerate(row) if r == source])
        value = held(source) if value is None else jnp.where(here, held(source), value)
    return value


def look_up(place, row):
    return sum(jnp.where(place == q, value, 0) for q, value in enumerate(row))


def after(value, *done):
    return lax.optimization_barrier((value, done))[0]


def local(
    latent,
    projections,
    frame_times,
    levels,
    gates,
    out_weight,
    incoming_latent,
    incoming_proj,
    incoming_times,
):
    place, count = lax.axis_index("queue"), lax.axis_size("queue")
    core, cores = lax.axis_index("seq"), lax.axis_size("seq")
    side, sides = lax.axis_index("heads"), lax.axis_size("heads")
    group, groups = lax.axis_index("groups"), lax.axis_size("groups")
    first, last = place == 0, place == count - 1
    frames, tokens, features = latent.shape
    channels = projections.shape[-1]
    assert cores == 2 and frames == 2 and groups == 2 and count % sides == 0
    columns = out_weight.shape[1]
    half = columns // 2
    swap = [(0, 1), (1, 0)]
    pair = ("queue", "seq")
    table = arrivals(count)
    block_of = [list(range(count))]
    for row in table:
        block_of.append([q + hops if way == "down" else q - hops for q, (way, hops) in enumerate(row)])

    depth = out_weight.shape[0] // 2
    cuts = [0, half]
    if half % HD == 0 and half > HD:
        cuts = [0, half - HD, half]
    chunks = list(zip(cuts[:-1], cuts[1:]))
    origin = lax.dynamic_slice(out_weight, (group * depth, core * half), (depth, half))
    whole = [(0, half)]
    held = {}

    def send_weights(name, block, low, hops, ends):
        for way, part, sign in (("up", block[0], 1), ("down", block[1], -1)):
            pairs = [(i, i + hops) for i in range(count - hops) if i >= ends]
            if sign < 0:
                pairs = [(count - 1 - i, count - 1 - j) for i, j in pairs]
            held[way, name, low] = lax.ppermute(part, "queue", pairs)

    gathered = {}

    def spread(k, low, high, *done):
        sources = {key: held[key + (0,)] for key in table[k - 1]}
        if done:
            sources = after(sources, *done)
        own = pick(place, table[k - 1], lambda key: sources[key][:, low:high])
        gathered[k, low] = (own, lax.ppermute(own, "groups", swap))
        return own

    send_weights(1, (origin, origin), 0, 1, 0)
    hop_1 = held["up", 1, 0], held["down", 1, 0]

    cos, sin = rotation_tables(jnp.concatenate([frame_times, incoming_times]))
    where = jnp.stack([core, first.astype(jnp.int32), last.astype(jnp.int32), levels[0]])
    mine, peer, peer_v, fresh = rotate_all(where, cos, sin, after(projections, origin), incoming_proj)
    got, got_v = lax.ppermute(peer, "seq", swap), lax.ppermute(peer_v, "seq", swap)
    back = [(i + 1, i) for i in range(count - 1)]
    far = lax.ppermute(after(bundle(where, mine, got, got_v), *hop_1), "queue", back)
    held["up", 1, 0], held["down", 1, 0] = hop_1
    spread(1, 0, half)
    if count > 2:
        send_weights(2, hop_1, 0, 1, 1)

    inputs = after((mine, got, got_v, fresh, far), gathered[1, 0][1])

    send, keep = attend(where, *inputs)
    came = lax.ppermute(send, "queue", back)
    next_level = after(far, came)[8 * tokens, :1].astype(jnp.int32)
    if count > 2:
        held["up", 2, 0], held["down", 2, 0] = after((held["up", 2, 0], held["down", 2, 0]), came)
    for hop in range(3, count):
        spread(hop - 1, 0, half)
        send_weights(hop, (held["up", hop - 1, 0], held["down", hop - 1, 0]), 0, 1, hop - 1)
    k = count - 1
    if keep.shape[1] < channels:
        peer_keep, peer_came = lax.ppermute(keep, "seq", swap), lax.ppermute(came, "seq", swap)
    else:
        peer_keep, peer_came = keep, came
    mix = keep, came, peer_keep, peer_came

    moved = lax.ppermute(after(latent, came), pair, [(i + 1, i) for i in range(2 * count - 1)])
    moved = jnp.where(jnp.logical_and(last, core == 1), incoming_latent, moved)
    moved = moved.reshape(frames * tokens, features)

    chosen = jnp.concatenate([levels, next_level])
    one_hot = (jnp.arange(gates.shape[0], dtype=jnp.int32)[None, :] == chosen[:, None]).astype(BF16)
    rows = jnp.dot(one_hot, gates, preferred_element_type=F32).astype(BF16)
    if sides == 2:
        other = lax.ppermute(rows, "heads", swap)
        rows = jnp.concatenate(
            [jnp.where(side == 0, rows, other), jnp.where(side == 0, other, rows)], axis=1
        )
    else:
        rows = lax.all_gather(rows, "heads", axis=1, tiled=True)
    rows = rows.astype(F32)
    crossing = jnp.where(last, 0.0, rows[1:2])
    gate_rows = jnp.concatenate([rows[:1], crossing], axis=0)

    per_side = count // sides
    flat = ("queue", "heads")

    def summed(k, pieces, low, *done):
        block = look_up(place, block_of[k])
        rows = after(mix, *done) if done else mix
        delta = project(group, core, half, block * columns + core * half + low, rows, pieces, gate_rows)
        if sides != 2:
            return block, delta, None
        pairs = [
            (q * 2 + 1 - block_of[k][q] // per_side, q * 2 + block_of[k][q] // per_side) for q in range(count)
        ]
        return block, delta, lax.ppermute(delta, flat, pairs)

    results, late, picked = [], [], []
    for n in range(k):
        pieces = [out_weight] if n == 0 else gathered[n, 0]
        if n == k - 1:
            for low, high in chunks:
                picked.append(spread(k, low, high, *picked, *[delta for _, delta, _ in results[-1:]]))
        results.append(summed(n, pieces, 0, *picked, *[delta for _, delta, _ in results[-1:]]))
    sums = [other for _, _, other in results if other is not None]
    for n, (low, _) in enumerate(chunks):
        done = [delta for _, delta, _ in results[-1:]] + [delta for _, (_, delta, _) in late]
        late.append((low, summed(k, gathered[k, low], low, *done, *(sums[2:] if n else sums[:2]))))
    if sides != 2:
        results += [result for _, result in late]
        change = jnp.zeros((2 * frames * tokens, count * half), BF16)
        for n, (block, delta, _) in enumerate(results):
            low = late[n - count + 1][0] if n >= count - 1 else 0
            change = lax.dynamic_update_slice_in_dim(change, delta, block * half + low, axis=1)
        early = lax.psum_scatter(change, "heads", scatter_dimension=1, tiled=True)
        late = []
    else:
        early = []
        for b in range(per_side):
            total = 0.0
            for block, delta, other in results:
                change = delta.astype(F32) + other.astype(F32)
                total = total + jnp.where(block == side * per_side + b, change, 0.0)
            early.append(total)
        early = jnp.concatenate(early, axis=1).astype(BF16)

    mine = frames * tokens
    early_back = lax.ppermute(early[mine:], "seq", swap)
    tail = []
    for low, (block, delta, other) in late:
        total = (delta.astype(F32) + other.astype(F32)).astype(BF16)
        tail.append((low, low + delta.shape[1], block, total[:mine], lax.ppermute(total[mine:], "seq", swap)))

    parts = []
    for b in range(per_side):
        for who in range(2):
            for low, high in chunks:
                at = b * half + low
                change = jnp.where(core == who, early[:mine, at : at + high - low], early_back[:, at : at + high - low])
                change = change.astype(F32)
                for start, _, block, own, back in tail:
                    if start == low:
                        last_part = jnp.where(core == who, own, back).astype(F32)
                        change = change + jnp.where(block == side * per_side + b, last_part, 0.0)
                at = b * columns + who * half + low
                parts.append((moved[:, at : at + high - low].astype(F32) + change).astype(BF16))
    return jnp.concatenate(parts, axis=1).reshape(frames, tokens, features)


def solution(mesh):
    return jax.shard_map(
        local,
        mesh=mesh,
        in_specs=(
            P(("groups", "queue", "seq"), None, "heads"),
            P(None, ("groups", "queue", "seq"), None, "heads"),
            P(("groups", "queue", "seq")),
            P(("groups", "queue")),
            P(None, "heads"),
            P("heads", "queue"),
            P("groups", None, "heads"),
            P("groups", None, None, "heads"),
            P("groups"),
        ),
        out_specs=P(("groups", "queue", "seq"), None, "heads"),
        check_vma=False,
    )
```

```python
import functools
import math

import jax
import jax.numpy as jnp
from jax import lax
from jax.experimental import pallas as pl
from jax.experimental.pallas import tpu as pltpu
from jax.sharding import PartitionSpec as P

HD = 128
BF16 = jnp.bfloat16
F32 = jnp.float32
SPARE = 16
VMEM_LIMIT = 16 * 1024 * 1024


COST = pl.CostEstimate(flops=1000, bytes_accessed=1000, transcendentals=0)


def params(*semantics):
    return pltpu.CompilerParams(dimension_semantics=semantics or None, vmem_limit_bytes=VMEM_LIMIT)


def rotation_tables(times):
    half = HD // 2
    pair_index = jnp.arange(half, dtype=F32)
    frequency = jnp.power(F32(10000.0), -pair_index / half)
    angles = times.astype(F32)[:, None] * frequency[None, :]
    cosine, sine = jnp.cos(angles), jnp.sin(angles)
    return (
        jnp.concatenate([cosine, cosine], axis=1),
        jnp.concatenate([-sine, sine], axis=1),
    )


def rotate_kernel(core_ref, cos_ref, sin_ref, own_ref, new_ref, mine_ref, peer_ref, peer_v_ref, fresh_ref):
    _, frames, _, channels = own_ref.shape
    share = mine_ref.shape[-1]

    def turn(block, row):
        block = block.astype(F32)
        out = block * cos_ref[row : row + 1, :] + pltpu.roll(block, HD // 2, 1) * sin_ref[row : row + 1, :]
        return out.astype(BF16)

    for head in range(share // HD):
        to = slice(head * HD, (head + 1) * HD)
        for target, core in ((mine_ref, core_ref[0]), (peer_ref, 1 - core_ref[0])):
            start = core * share if share < channels else 0
            at = pl.ds(pl.multiple_of(start + head * HD, HD), HD)
            for frame in range(frames):
                target[0, frame, :, to] = turn(own_ref[0, frame, :, at], frame)
                target[1, frame, :, to] = turn(own_ref[1, frame, :, at], frame)
                if target is mine_ref:
                    target[2, frame, :, to] = own_ref[2, frame, :, at]
                else:
                    peer_v_ref[frame, :, to] = own_ref[2, frame, :, at]
        start = core_ref[0] * share if share < channels else 0
        at = pl.ds(pl.multiple_of(start + head * HD, HD), HD)
        for frame in range(frames):
            fresh_ref[0, frame, :, to] = turn(new_ref[frame, 0, :, at], frames + frame)
            fresh_ref[1, frame, :, to] = turn(new_ref[frame, 1, :, at], frames + frame)
            fresh_ref[2, frame, :, to] = new_ref[frame, 2, :, at]

def rotate_all(where, cos, sin, own, new):
    _, frames, tokens, channels = own.shape
    share = channels // 2 if channels % (2 * HD) == 0 else channels
    full = jax.ShapeDtypeStruct((3, frames, tokens, share), BF16)
    return pl.pallas_call(
        rotate_kernel,
        in_specs=[pl.BlockSpec(memory_space=pltpu.SMEM)] + [pl.BlockSpec(memory_space=pltpu.VMEM)] * 4,
        out_specs=[pl.BlockSpec(memory_space=pltpu.VMEM)] * 4,
        out_shape=[
            full,
            jax.ShapeDtypeStruct((2, frames, tokens, share), BF16),
            jax.ShapeDtypeStruct((frames, tokens, share), BF16),
            full,
        ],
        compiler_params=params(),
        cost_estimate=COST,
        name="rotate",
    )(where, cos, sin, own, new)


def bundle_kernel(where_ref, mine, got, got_v, out_ref):
    theirs = got.at[0], got.at[1], got_v
    tokens = mine.shape[2]
    second_core = where_ref[0] == 1
    for kind in range(3):
        for frame in range(2):
            at = (2 * kind + frame) * tokens
            out_ref[at : at + tokens, :] = jnp.where(second_core, theirs[kind][frame], mine[kind, frame])
    for kind in (1, 2):
        at = (5 + kind) * tokens
        out_ref[at : at + tokens, :] = jnp.where(second_core, mine[kind, 0], theirs[kind][0])
    level = jnp.full((SPARE, out_ref.shape[1]), where_ref[3].astype(F32))
    out_ref[8 * tokens :, :] = level.astype(BF16)


def bundle(where, mine, got, got_v):
    _, _, tokens, share = mine.shape
    return pl.pallas_call(
        bundle_kernel,
        in_specs=[pl.BlockSpec(memory_space=pltpu.SMEM)] + [pl.BlockSpec(memory_space=pltpu.VMEM)] * 3,
        out_specs=pl.BlockSpec(memory_space=pltpu.VMEM),
        out_shape=jax.ShapeDtypeStruct((8 * tokens + SPARE, share), BF16),
        compiler_params=params(),
        cost_estimate=COST,
        name="bundle",
    )(where, mine, got, got_v)


def attend_kernel(where_ref, mine, got, got_v, fresh, far_ref, send_ref, keep_ref):
    theirs = got.at[0], got.at[1], got_v
    tokens = mine.shape[2]
    heads = mine.shape[-1] // HD
    core, first, last = where_ref[0], where_ref[1] == 1, where_ref[2] == 1
    second_core = core == 1
    factor = math.log2(math.e) / math.sqrt(HD)

    def one(at):
        def frames_of(kind):
            own = [mine[kind, frame, :, at] for frame in range(2)]
            peer = [theirs[kind][frame, :, at] for frame in range(2)]
            rows = [jnp.where(second_core, p, o) for o, p in zip(own, peer)]
            rows += [jnp.where(second_core, o, p) for o, p in zip(own, peer)]
            for frame in range(2):
                far = far_ref[(2 * kind + frame) * tokens : (2 * kind + frame + 1) * tokens, at]
                rows.append(jnp.where(last, fresh[kind, frame, :, at], far))
            if kind:
                rows.append(far_ref[(5 + kind) * tokens : (6 + kind) * tokens, at])
            return rows

        queries, keys, values = frames_of(0), frames_of(1), frames_of(2)

        def mix(query, low):
            rows = lax.dot_general(
                jnp.concatenate(query, axis=0),
                jnp.concatenate(keys[low : low + 6], axis=0),
                (((1,), (1,)), ((), ())),
                preferred_element_type=F32,
            )
            part = [rows[:, i * tokens : (i + 1) * tokens] for i in range(6)]
            part[0] = jnp.where(first, -1e30, part[0])
            part[5] = jnp.where(last, -1e30, part[5])
            rows = jnp.concatenate(part, axis=1)
            top = jnp.max(rows, axis=1, keepdims=True)
            weights = jnp.exp2((rows - top) * factor)
            total = jnp.sum(weights, axis=1, keepdims=True)
            out = jnp.dot(
                weights.astype(BF16),
                jnp.concatenate(values[low : low + 6], axis=0),
                preferred_element_type=F32,
            )
            return (out * (1.0 / total)).astype(BF16)

        early = mix(queries[1:5], 0)
        send_ref[:, at] = early[:tokens]
        keep_ref[: 3 * tokens, at] = early[tokens:]
        keep_ref[3 * tokens :, at] = mix(queries[2:6], 1)

    group = 3 if heads % 3 == 0 else 1

    @pl.loop(0, heads // group)
    def _(step):
        for head in range(group):
            one(pl.ds(pl.multiple_of((step * group + head) * HD, HD), HD))


def attend(where, *operands):
    _, _, tokens, share = operands[0].shape
    return pl.pallas_call(
        attend_kernel,
        in_specs=[pl.BlockSpec(memory_space=pltpu.SMEM)] + [pl.BlockSpec(memory_space=pltpu.VMEM)] * len(operands),
        out_specs=[pl.BlockSpec(memory_space=pltpu.VMEM)] * 2,
        out_shape=[
            jax.ShapeDtypeStruct((tokens, share), BF16),
            jax.ShapeDtypeStruct((7 * tokens, share), BF16),
        ],
        compiler_params=params(),
        cost_estimate=COST,
        name="attend",
    )(where, *operands)


def project_kernel(half, place_ref, keep_ref, came_ref, peer_keep_ref, peer_came_ref, gate_ref, *refs):
    pieces, out_ref = refs[:-1], refs[-1]
    group, core, gate_at = place_ref[0], place_ref[1], place_ref[2]
    tokens, depth = came_ref.shape
    own = jnp.concatenate([keep_ref[...], came_ref[...]], axis=0)
    peer = jnp.concatenate([peer_keep_ref[...], peer_came_ref[...]], axis=0)
    if len(pieces) == 1:
        widths = [256] * (half // 256) + [half % 256] * (half % 256 > 0)
    else:
        widths = [piece.shape[1] for piece in pieces[::2]]
    low = 0
    for i, wide in enumerate(widths):
        if len(pieces) == 1:
            at = pl.ds(pl.multiple_of(core * half + low, HD), wide)
            near = pieces[0][pl.ds(pl.multiple_of(core * depth, HD), depth), at]
            far = pieces[0][pl.ds(pl.multiple_of((1 - core) * depth, HD), depth), at]
        else:
            here, there = pieces[2 * i][...], pieces[2 * i + 1][...]
            near = jnp.where(group == core, here, there)
            far = jnp.where(group == core, there, here)
        total = jnp.dot(own, near, preferred_element_type=F32)
        total = total + jnp.dot(peer, far, preferred_element_type=F32)
        at = pl.ds(pl.multiple_of(gate_at + low, HD), wide)
        row, crossing = gate_ref[0:1, at], gate_ref[1:2, at]
        order = (0, 1, 2, 7, 3, 4, 5, 6)
        parts = [total[n * tokens : (n + 1) * tokens] for n in order]
        for who in range(2):
            base = jnp.where(core == who, 0, 2 * tokens)
            for frame in range(2):
                n = 2 * who + frame
                gate = crossing if n == 3 else row
                result = (parts[n] * gate + parts[4 + n] * row).astype(BF16)
                out_ref[pl.ds(pl.multiple_of(base + frame * tokens, tokens), tokens), low : low + wide] = result
        low += wide


def project(group, core, half, gate_at, mix, pieces, gates):
    keep, came, peer_keep, peer_came = mix
    tokens, share = came.shape
    columns = half if len(pieces) == 1 else sum(piece.shape[1] for piece in pieces[::2])
    if 2 * share != pieces[0].shape[0] * (1 if len(pieces) == 1 else 2) or share % HD or half % HD:
        if len(pieces) == 1:
            weights = lax.dynamic_slice_in_dim(pieces[0], core * half, half, axis=1)
        else:
            weights = [
                jnp.where(group == 0, jnp.concatenate([own, other]), jnp.concatenate([other, own]))
                for own, other in zip(pieces[::2], pieces[1::2])
            ]
            weights = jnp.concatenate(weights, axis=1)
        rows = jnp.concatenate([keep, came], axis=0)
        if 2 * share == weights.shape[0]:
            peer = jnp.concatenate([peer_keep, peer_came], axis=0)
            rows = jnp.where(
                core == 0, jnp.concatenate([rows, peer], axis=1), jnp.concatenate([peer, rows], axis=1)
            )
        total = jnp.dot(rows, weights, preferred_element_type=F32).reshape(8, tokens, columns)
        gates = lax.dynamic_slice_in_dim(gates, gate_at, columns, axis=1)
        first = jnp.stack([total[0], total[1], total[2], total[7]])
        scale = jnp.stack([gates[0], gates[0], gates[0], gates[1]])[:, None, :]
        total = (first * scale + total[3:7] * gates[0]).reshape(2, 2 * tokens, columns)
        total = jnp.where(core == 0, total, total[::-1])
        return total.reshape(4 * tokens, columns).astype(BF16)

    place = jnp.stack([group, core, gate_at]).astype(jnp.int32)
    return pl.pallas_call(
        functools.partial(project_kernel, half),
        in_specs=[pl.BlockSpec(memory_space=pltpu.SMEM)]
        + [pl.BlockSpec(memory_space=pltpu.VMEM)] * (5 + len(pieces)),
        out_specs=pl.BlockSpec(memory_space=pltpu.VMEM),
        out_shape=jax.ShapeDtypeStruct((4 * tokens, columns), BF16),
        compiler_params=params(),
        cost_estimate=COST,
        name="project",
    )(place, *mix, gates, *pieces)


def arrivals(count):
    table = []
    for k in range(1, count):
        row = []
        for q in range(count):
            ahead, behind = count - 1 - q, q
            if q < count // 2:
                row.append(("down", k) if k <= ahead else ("up", k - ahead))
            else:
                row.append(("up", k) if k <= behind else ("down", k - behind))
        table.append(row)
    return table


def pick(place, row, held):
    value = None
    for source in sorted(set(row)):
        here = functools.reduce(jnp.logical_or, [place == q for q, r in enumerate(row) if r == source])
        value = held(source) if value is None else jnp.where(here, held(source), value)
    return value


def look_up(place, row):
    return sum(jnp.where(place == q, value, 0) for q, value in enumerate(row))


def after(value, *done):
    return lax.optimization_barrier((value, done))[0]


def local(
    latent,
    projections,
    frame_times,
    levels,
    gates,
    out_weight,
    incoming_latent,
    incoming_proj,
    incoming_times,
):
    place, count = lax.axis_index("queue"), lax.axis_size("queue")
    core, cores = lax.axis_index("seq"), lax.axis_size("seq")
    side, sides = lax.axis_index("heads"), lax.axis_size("heads")
    group, groups = lax.axis_index("groups"), lax.axis_size("groups")
    first, last = place == 0, place == count - 1
    frames, tokens, features = latent.shape
    channels = projections.shape[-1]
    assert cores == 2 and frames == 2 and groups == 2 and count % sides == 0
    columns = out_weight.shape[1]
    half = columns // 2
    swap = [(0, 1), (1, 0)]
    pair = ("queue", "seq")
    table = arrivals(count)
    block_of = [list(range(count))]
    for row in table:
        block_of.append([q + hops if way == "down" else q - hops for q, (way, hops) in enumerate(row)])

    depth = out_weight.shape[0] // 2
    cuts = [0, half]
    if half % HD == 0 and half > HD:
        cuts = [0, half - HD, half]
    chunks = list(zip(cuts[:-1], cuts[1:]))
    origin = lax.dynamic_slice(out_weight, (group * depth, core * half), (depth, half))
    whole = [(0, half)]
    held = {}

    def send_weights(name, block, low, hops, ends):
        for way, part, sign in (("down", block[1], -1), ("up", block[0], 1)):
            pairs = [(i, i + hops) for i in range(count - hops) if i >= ends]
            if sign < 0:
                pairs = [(count - 1 - i, count - 1 - j) for i, j in pairs]
            held[way, name, low] = lax.ppermute(part, "queue", pairs)

    gathered = {}

    def spread(k, low, high, *done):
        sources = {key: held[key + (0,)] for key in table[k - 1]}
        if done:
            sources = after(sources, *done)
        own = pick(place, table[k - 1], lambda key: sources[key][:, low:high])
        gathered[k, low] = (own, lax.ppermute(own, "groups", swap))
        return own

    send_weights(1, (origin, origin), 0, 1, 0)
    hop_1 = held["up", 1, 0], held["down", 1, 0]

    cos, sin = rotation_tables(jnp.concatenate([frame_times, incoming_times]))
    where = jnp.stack([core, first.astype(jnp.int32), last.astype(jnp.int32), levels[0]])
    mine, peer, peer_v, fresh = rotate_all(where, cos, sin, after(projections, origin), incoming_proj)
    got, got_v = lax.ppermute(peer, "seq", swap), lax.ppermute(peer_v, "seq", swap)
    back = [(i + 1, i) for i in range(count - 1)]
    far = lax.ppermute(after(bundle(where, mine, got, got_v), *hop_1), "queue", back)
    held["up", 1, 0], held["down", 1, 0] = hop_1
    spread(1, 0, half)
    if count > 2:
        send_weights(2, hop_1, 0, 1, 1)

    inputs = after((mine, got, got_v, fresh, far), gathered[1, 0][1])

    send, keep = attend(where, *inputs)
    came = lax.ppermute(send, "queue", back)
    next_level = after(far, came)[8 * tokens, :1].astype(jnp.int32)
    if count > 2:
        held["up", 2, 0], held["down", 2, 0] = after((held["up", 2, 0], held["down", 2, 0]), came)
    for hop in range(3, count):
        spread(hop - 1, 0, half)
        send_weights(hop, (held["up", hop - 1, 0], held["down", hop - 1, 0]), 0, 1, hop - 1)
    k = count - 1
    if keep.shape[1] < channels:
        peer_keep, peer_came = lax.ppermute(keep, "seq", swap), lax.ppermute(came, "seq", swap)
    else:
        peer_keep, peer_came = keep, came
    mix = keep, came, peer_keep, peer_came

    moved = lax.ppermute(after(latent, came), pair, [(i + 1, i) for i in range(2 * count - 1)])
    moved = jnp.where(jnp.logical_and(last, core == 1), incoming_latent, moved)
    moved = moved.reshape(frames * tokens, features)

    chosen = jnp.concatenate([levels, next_level])
    one_hot = (jnp.arange(gates.shape[0], dtype=jnp.int32)[None, :] == chosen[:, None]).astype(BF16)
    rows = jnp.dot(one_hot, gates, preferred_element_type=F32).astype(BF16)
    if sides == 2:
        other = lax.ppermute(rows, "heads", swap)
        rows = jnp.concatenate(
            [jnp.where(side == 0, rows, other), jnp.where(side == 0, other, rows)], axis=1
        )
    else:
        rows = lax.all_gather(rows, "heads", axis=1, tiled=True)
    rows = rows.astype(F32)
    crossing = jnp.where(last, 0.0, rows[1:2])
    gate_rows = jnp.concatenate([rows[:1], crossing], axis=0)

    per_side = count // sides
    flat = ("queue", "heads")

    def summed(k, pieces, low, *done):
        block = look_up(place, block_of[k])
        rows = after(mix, *done) if done else mix
        delta = project(group, core, half, block * columns + core * half + low, rows, pieces, gate_rows)
        if sides != 2:
            return block, delta, None
        pairs = [
            (q * 2 + 1 - block_of[k][q] // per_side, q * 2 + block_of[k][q] // per_side) for q in range(count)
        ]
        return block, delta, lax.ppermute(delta, flat, pairs)

    results, late, picked = [], [], []
    for n in [1, 0][2 - min(k, 2) :] + list(range(2, k)):
        pieces = [out_weight] if n == 0 else gathered[n, 0]
        if n == k - 1:
            for low, high in chunks:
                picked.append(spread(k, low, high, *picked, *[delta for _, delta, _ in results[-1:]]))
        results.append(summed(n, pieces, 0, *picked, *[delta for _, delta, _ in results[-1:]]))
    sums = [other for _, _, other in results if other is not None]
    for n, (low, _) in enumerate(chunks):
        done = [delta for _, delta, _ in results[-1:]] + [delta for _, (_, delta, _) in late]
        late.append((low, summed(k, gathered[k, low], low, *done, *(sums[2:] if n else sums[:2]))))
    if sides != 2:
        results += [result for _, result in late]
        change = jnp.zeros((2 * frames * tokens, count * half), BF16)
        for n, (block, delta, _) in enumerate(results):
            low = late[n - count + 1][0] if n >= count - 1 else 0
            change = lax.dynamic_update_slice_in_dim(change, delta, block * half + low, axis=1)
        early = lax.psum_scatter(change, "heads", scatter_dimension=1, tiled=True)
        late = []
    else:
        early = []
        for b in range(per_side):
            total = 0.0
            for block, delta, other in results:
                change = delta.astype(F32) + other.astype(F32)
                total = total + jnp.where(block == side * per_side + b, change, 0.0)
            early.append(total)
        early = jnp.concatenate(early, axis=1).astype(BF16)

    mine = frames * tokens
    early_back = lax.ppermute(early[mine:], "seq", swap)
    tail = []
    for low, (block, delta, other) in late:
        total = (delta.astype(F32) + other.astype(F32)).astype(BF16)
        tail.append((low, low + delta.shape[1], block, total[:mine], lax.ppermute(total[mine:], "seq", swap)))

    parts = []
    for b in range(per_side):
        for who in range(2):
            for low, high in chunks:
                at = b * half + low
                change = jnp.where(core == who, early[:mine, at : at + high - low], early_back[:, at : at + high - low])
                change = change.astype(F32)
                for start, _, block, own, back in tail:
                    if start == low:
                        last_part = jnp.where(core == who, own, back).astype(F32)
                        change = change + jnp.where(block == side * per_side + b, last_part, 0.0)
                at = b * columns + who * half + low
                parts.append((moved[:, at : at + high - low].astype(F32) + change).astype(BF16))
    return jnp.concatenate(parts, axis=1).reshape(frames, tokens, features)


def solution(mesh):
    return jax.shard_map(
        local,
        mesh=mesh,
        in_specs=(
            P(("groups", "queue", "seq"), None, "heads"),
            P(None, ("groups", "queue", "seq"), None, "heads"),
            P(("groups", "queue", "seq")),
            P(("groups", "queue")),
            P(None, "heads"),
            P("heads", "queue"),
            P("groups", None, "heads"),
            P("groups", None, None, "heads"),
            P("groups"),
        ),
        out_specs=P(("groups", "queue", "seq"), None, "heads"),
        check_vma=False,
    )
```

```python
import functools
import math

import jax
import jax.numpy as jnp
from jax import lax
from jax.experimental import pallas as pl
from jax.experimental.pallas import tpu as pltpu
from jax.sharding import PartitionSpec as P

HD = 128
BF16 = jnp.bfloat16
F32 = jnp.float32
SPARE = 16
VMEM_LIMIT = 16 * 1024 * 1024


COST = pl.CostEstimate(flops=1000, bytes_accessed=1000, transcendentals=0)


def params(*semantics):
    return pltpu.CompilerParams(dimension_semantics=semantics or None, vmem_limit_bytes=VMEM_LIMIT)


def rotation_tables(times):
    half = HD // 2
    pair_index = jnp.arange(half, dtype=F32)
    frequency = jnp.power(F32(10000.0), -pair_index / half)
    angles = times.astype(F32)[:, None] * frequency[None, :]
    cosine, sine = jnp.cos(angles), jnp.sin(angles)
    return (
        jnp.concatenate([cosine, cosine], axis=1),
        jnp.concatenate([-sine, sine], axis=1),
    )


def rotate_kernel(core_ref, cos_ref, sin_ref, own_ref, new_ref, mine_ref, peer_ref, peer_v_ref, fresh_ref):
    _, frames, _, channels = own_ref.shape
    share = mine_ref.shape[-1]

    def turn(block, row):
        block = block.astype(F32)
        out = block * cos_ref[row : row + 1, :] + pltpu.roll(block, HD // 2, 1) * sin_ref[row : row + 1, :]
        return out.astype(BF16)

    for head in range(share // HD):
        to = slice(head * HD, (head + 1) * HD)
        for target, core in ((mine_ref, core_ref[0]), (peer_ref, 1 - core_ref[0])):
            start = core * share if share < channels else 0
            at = pl.ds(pl.multiple_of(start + head * HD, HD), HD)
            for frame in range(frames):
                target[0, frame, :, to] = turn(own_ref[0, frame, :, at], frame)
                target[1, frame, :, to] = turn(own_ref[1, frame, :, at], frame)
                if target is mine_ref:
                    target[2, frame, :, to] = own_ref[2, frame, :, at]
                else:
                    peer_v_ref[frame, :, to] = own_ref[2, frame, :, at]
        start = core_ref[0] * share if share < channels else 0
        at = pl.ds(pl.multiple_of(start + head * HD, HD), HD)
        for frame in range(frames):
            fresh_ref[0, frame, :, to] = turn(new_ref[frame, 0, :, at], frames + frame)
            fresh_ref[1, frame, :, to] = turn(new_ref[frame, 1, :, at], frames + frame)
            fresh_ref[2, frame, :, to] = new_ref[frame, 2, :, at]

def rotate_all(where, cos, sin, own, new):
    _, frames, tokens, channels = own.shape
    share = channels // 2 if channels % (2 * HD) == 0 else channels
    full = jax.ShapeDtypeStruct((3, frames, tokens, share), BF16)
    return pl.pallas_call(
        rotate_kernel,
        in_specs=[pl.BlockSpec(memory_space=pltpu.SMEM)] + [pl.BlockSpec(memory_space=pltpu.VMEM)] * 4,
        out_specs=[pl.BlockSpec(memory_space=pltpu.VMEM)] * 4,
        out_shape=[
            full,
            jax.ShapeDtypeStruct((2, frames, tokens, share), BF16),
            jax.ShapeDtypeStruct((frames, tokens, share), BF16),
            full,
        ],
        compiler_params=params(),
        cost_estimate=COST,
        name="rotate",
    )(where, cos, sin, own, new)


def bundle_kernel(where_ref, mine, got, got_v, out_ref):
    theirs = got.at[0], got.at[1], got_v
    tokens = mine.shape[2]
    second_core = where_ref[0] == 1
    for kind in range(3):
        for frame in range(2):
            at = (2 * kind + frame) * tokens
            out_ref[at : at + tokens, :] = jnp.where(second_core, theirs[kind][frame], mine[kind, frame])
    for kind in (1, 2):
        at = (5 + kind) * tokens
        out_ref[at : at + tokens, :] = jnp.where(second_core, mine[kind, 0], theirs[kind][0])
    level = jnp.full((SPARE, out_ref.shape[1]), where_ref[3].astype(F32))
    out_ref[8 * tokens :, :] = level.astype(BF16)


def bundle(where, mine, got, got_v):
    _, _, tokens, share = mine.shape
    return pl.pallas_call(
        bundle_kernel,
        in_specs=[pl.BlockSpec(memory_space=pltpu.SMEM)] + [pl.BlockSpec(memory_space=pltpu.VMEM)] * 3,
        out_specs=pl.BlockSpec(memory_space=pltpu.VMEM),
        out_shape=jax.ShapeDtypeStruct((8 * tokens + SPARE, share), BF16),
        compiler_params=params(),
        cost_estimate=COST,
        name="bundle",
    )(where, mine, got, got_v)


def attend_kernel(where_ref, mine, got, got_v, fresh, far_ref, gate_ref, send_ref, keep_ref, row_ref):
    theirs = got.at[0], got.at[1], got_v
    tokens = mine.shape[2]
    heads = mine.shape[-1] // HD
    core, first, last = where_ref[0], where_ref[1] == 1, where_ref[2] == 1
    second_core = core == 1
    factor = math.log2(math.e) / math.sqrt(HD)

    def one(at):
        def frames_of(kind):
            own = [mine[kind, frame, :, at] for frame in range(2)]
            peer = [theirs[kind][frame, :, at] for frame in range(2)]
            rows = [jnp.where(second_core, p, o) for o, p in zip(own, peer)]
            rows += [jnp.where(second_core, o, p) for o, p in zip(own, peer)]
            for frame in range(2):
                far = far_ref[(2 * kind + frame) * tokens : (2 * kind + frame + 1) * tokens, at]
                rows.append(jnp.where(last, fresh[kind, frame, :, at], far))
            if kind:
                rows.append(far_ref[(5 + kind) * tokens : (6 + kind) * tokens, at])
            return rows

        queries, keys, values = frames_of(0), frames_of(1), frames_of(2)

        def mix(query, low):
            rows = lax.dot_general(
                jnp.concatenate(query, axis=0),
                jnp.concatenate(keys[low : low + 6], axis=0),
                (((1,), (1,)), ((), ())),
                preferred_element_type=F32,
            )
            part = [rows[:, i * tokens : (i + 1) * tokens] for i in range(6)]
            part[0] = jnp.where(first, -1e30, part[0])
            part[5] = jnp.where(last, -1e30, part[5])
            rows = jnp.concatenate(part, axis=1)
            top = jnp.max(rows, axis=1, keepdims=True)
            weights = jnp.exp2((rows - top) * factor)
            total = jnp.sum(weights, axis=1, keepdims=True)
            out = jnp.dot(
                weights.astype(BF16),
                jnp.concatenate(values[low : low + 6], axis=0),
                preferred_element_type=F32,
            )
            return (out * (1.0 / total)).astype(BF16)

        early = mix(queries[1:5], 0)
        send_ref[:, at] = early[:tokens]
        keep_ref[: 3 * tokens, at] = early[tokens:]
        keep_ref[3 * tokens :, at] = mix(queries[2:6], 1)

    level = far_ref[8 * tokens : 8 * tokens + SPARE, :HD].astype(F32)[0:1]
    for at in range(0, gate_ref.shape[1], HD):
        rows = gate_ref[:, at : at + HD]
        chosen = lax.broadcasted_iota(jnp.int32, rows.shape, 0).astype(F32) == level
        row_ref[:, at : at + HD] = jnp.sum(jnp.where(chosen, rows, 0.0), axis=0, keepdims=True)

    group = 3 if heads % 3 == 0 else 1

    @pl.loop(0, heads // group)
    def _(step):
        for head in range(group):
            one(pl.ds(pl.multiple_of((step * group + head) * HD, HD), HD))


def attend(where, *operands):
    _, _, tokens, share = operands[0].shape
    return pl.pallas_call(
        attend_kernel,
        in_specs=[pl.BlockSpec(memory_space=pltpu.SMEM)] + [pl.BlockSpec(memory_space=pltpu.VMEM)] * len(operands),
        out_specs=[pl.BlockSpec(memory_space=pltpu.VMEM)] * 3,
        out_shape=[
            jax.ShapeDtypeStruct((tokens, share), BF16),
            jax.ShapeDtypeStruct((7 * tokens, share), BF16),
            jax.ShapeDtypeStruct((1, operands[-1].shape[1]), F32),
        ],
        compiler_params=params(),
        cost_estimate=COST,
        name="attend",
    )(where, *operands)


def project_kernel(half, place_ref, keep_ref, came_ref, peer_keep_ref, peer_came_ref, gate_ref, *refs):
    pieces, out_ref = refs[:-1], refs[-1]
    group, core, gate_at = place_ref[0], place_ref[1], place_ref[2]
    tokens, depth = came_ref.shape
    own = jnp.concatenate([keep_ref[...], came_ref[...]], axis=0)
    peer = jnp.concatenate([peer_keep_ref[...], peer_came_ref[...]], axis=0)
    if len(pieces) == 1:
        widths = [256] * (half // 256) + [half % 256] * (half % 256 > 0)
    else:
        widths = [piece.shape[1] for piece in pieces[::2]]
    low = 0
    for i, wide in enumerate(widths):
        if len(pieces) == 1:
            at = pl.ds(pl.multiple_of(core * half + low, HD), wide)
            near = pieces[0][pl.ds(pl.multiple_of(core * depth, HD), depth), at]
            far = pieces[0][pl.ds(pl.multiple_of((1 - core) * depth, HD), depth), at]
        else:
            here, there = pieces[2 * i][...], pieces[2 * i + 1][...]
            near = jnp.where(group == core, here, there)
            far = jnp.where(group == core, there, here)
        total = jnp.dot(own, near, preferred_element_type=F32)
        total = total + jnp.dot(peer, far, preferred_element_type=F32)
        at = pl.ds(pl.multiple_of(gate_at + low, HD), wide)
        row, crossing = gate_ref[0:1, at], gate_ref[1:2, at]
        order = (0, 1, 2, 7, 3, 4, 5, 6)
        parts = [total[n * tokens : (n + 1) * tokens] for n in order]
        for who in range(2):
            base = jnp.where(core == who, 0, 2 * tokens)
            for frame in range(2):
                n = 2 * who + frame
                gate = crossing if n == 3 else row
                result = (parts[n] * gate + parts[4 + n] * row).astype(BF16)
                out_ref[pl.ds(pl.multiple_of(base + frame * tokens, tokens), tokens), low : low + wide] = result
        low += wide


def project(group, core, half, gate_at, mix, pieces, gates):
    keep, came, peer_keep, peer_came = mix
    tokens, share = came.shape
    columns = half if len(pieces) == 1 else sum(piece.shape[1] for piece in pieces[::2])
    if 2 * share != pieces[0].shape[0] * (1 if len(pieces) == 1 else 2) or share % HD or half % HD:
        if len(pieces) == 1:
            weights = lax.dynamic_slice_in_dim(pieces[0], core * half, half, axis=1)
        else:
            weights = [
                jnp.where(group == 0, jnp.concatenate([own, other]), jnp.concatenate([other, own]))
                for own, other in zip(pieces[::2], pieces[1::2])
            ]
            weights = jnp.concatenate(weights, axis=1)
        rows = jnp.concatenate([keep, came], axis=0)
        if 2 * share == weights.shape[0]:
            peer = jnp.concatenate([peer_keep, peer_came], axis=0)
            rows = jnp.where(
                core == 0, jnp.concatenate([rows, peer], axis=1), jnp.concatenate([peer, rows], axis=1)
            )
        total = jnp.dot(rows, weights, preferred_element_type=F32).reshape(8, tokens, columns)
        gates = lax.dynamic_slice_in_dim(gates, gate_at, columns, axis=1)
        first = jnp.stack([total[0], total[1], total[2], total[7]])
        scale = jnp.stack([gates[0], gates[0], gates[0], gates[1]])[:, None, :]
        total = (first * scale + total[3:7] * gates[0]).reshape(2, 2 * tokens, columns)
        total = jnp.where(core == 0, total, total[::-1])
        return total.reshape(4 * tokens, columns).astype(BF16)

    place = jnp.stack([group, core, gate_at]).astype(jnp.int32)
    return pl.pallas_call(
        functools.partial(project_kernel, half),
        in_specs=[pl.BlockSpec(memory_space=pltpu.SMEM)]
        + [pl.BlockSpec(memory_space=pltpu.VMEM)] * (5 + len(pieces)),
        out_specs=pl.BlockSpec(memory_space=pltpu.VMEM),
        out_shape=jax.ShapeDtypeStruct((4 * tokens, columns), BF16),
        compiler_params=params(),
        cost_estimate=COST,
        name="project",
    )(place, *mix, gates, *pieces)


def arrivals(count):
    table = []
    for k in range(1, count):
        row = []
        for q in range(count):
            ahead, behind = count - 1 - q, q
            if q < count // 2:
                row.append(("down", k) if k <= ahead else ("up", k - ahead))
            else:
                row.append(("up", k) if k <= behind else ("down", k - behind))
        table.append(row)
    return table


def pick(place, row, held):
    value = None
    for source in sorted(set(row)):
        here = functools.reduce(jnp.logical_or, [place == q for q, r in enumerate(row) if r == source])
        value = held(source) if value is None else jnp.where(here, held(source), value)
    return value


def look_up(place, row):
    return sum(jnp.where(place == q, value, 0) for q, value in enumerate(row))


def after(value, *done):
    return lax.optimization_barrier((value, done))[0]


def local(
    latent,
    projections,
    frame_times,
    levels,
    gates,
    out_weight,
    incoming_latent,
    incoming_proj,
    incoming_times,
):
    place, count = lax.axis_index("queue"), lax.axis_size("queue")
    core, cores = lax.axis_index("seq"), lax.axis_size("seq")
    side, sides = lax.axis_index("heads"), lax.axis_size("heads")
    group, groups = lax.axis_index("groups"), lax.axis_size("groups")
    first, last = place == 0, place == count - 1
    frames, tokens, features = latent.shape
    channels = projections.shape[-1]
    assert cores == 2 and frames == 2 and groups == 2 and count % sides == 0
    columns = out_weight.shape[1]
    half = columns // 2
    swap = [(0, 1), (1, 0)]
    pair = ("queue", "seq")
    table = arrivals(count)
    block_of = [list(range(count))]
    for row in table:
        block_of.append([q + hops if way == "down" else q - hops for q, (way, hops) in enumerate(row)])

    depth = out_weight.shape[0] // 2
    cuts = [0, half]
    if half % HD == 0 and half > HD:
        cuts = [0, half - HD, half]
    chunks = list(zip(cuts[:-1], cuts[1:]))
    origin = lax.dynamic_slice(out_weight, (group * depth, core * half), (depth, half))
    whole = [(0, half)]
    held = {}

    def send_weights(name, block, low, hops, ends):
        for way, part, sign in (("down", block[1], -1), ("up", block[0], 1)):
            pairs = [(i, i + hops) for i in range(count - hops) if i >= ends]
            if sign < 0:
                pairs = [(count - 1 - i, count - 1 - j) for i, j in pairs]
            held[way, name, low] = lax.ppermute(part, "queue", pairs)

    gathered = {}

    def spread(k, low, high, *done):
        sources = {key: held[key + (0,)] for key in table[k - 1]}
        if done:
            sources = after(sources, *done)
        own = pick(place, table[k - 1], lambda key: sources[key][:, low:high])
        gathered[k, low] = (own, lax.ppermute(own, "groups", swap))
        return own

    send_weights(1, (origin, origin), 0, 1, 0)
    hop_1 = held["up", 1, 0], held["down", 1, 0]

    cos, sin = rotation_tables(jnp.concatenate([frame_times, incoming_times]))
    where = jnp.stack([core, first.astype(jnp.int32), last.astype(jnp.int32), levels[0]])
    mine, peer, peer_v, fresh = rotate_all(where, cos, sin, after(projections, origin), incoming_proj)
    got, got_v = lax.ppermute(peer, "seq", swap), lax.ppermute(peer_v, "seq", swap)
    back = [(i + 1, i) for i in range(count - 1)]
    far = lax.ppermute(after(bundle(where, mine, got, got_v), *hop_1), "queue", back)
    held["up", 1, 0], held["down", 1, 0] = hop_1
    spread(1, 0, half)
    if count > 2:
        send_weights(2, hop_1, 0, 1, 1)

    inputs = after((mine, got, got_v, fresh, far), gathered[1, 0][1])

    table_of_gates = jnp.pad(gates.astype(F32), ((0, -gates.shape[0] % 8), (0, 0)))
    send, keep, next_row = attend(where, *inputs, table_of_gates)
    came = lax.ppermute(send, "queue", back)
    if count > 2:
        held["up", 2, 0], held["down", 2, 0] = after((held["up", 2, 0], held["down", 2, 0]), came)
    for hop in range(3, count):
        spread(hop - 1, 0, half)
        send_weights(hop, (held["up", hop - 1, 0], held["down", hop - 1, 0]), 0, 1, hop - 1)
    k = count - 1
    if keep.shape[1] < channels:
        peer_keep, peer_came = lax.ppermute(keep, "seq", swap), lax.ppermute(came, "seq", swap)
    else:
        peer_keep, peer_came = keep, came
    mix = keep, came, peer_keep, peer_came

    moved = lax.ppermute(after(latent, came), pair, [(i + 1, i) for i in range(2 * count - 1)])
    moved = jnp.where(jnp.logical_and(last, core == 1), incoming_latent, moved)
    moved = moved.reshape(frames * tokens, features)

    one_hot = (jnp.arange(gates.shape[0], dtype=jnp.int32) == levels[0]).astype(BF16)[None, :]
    own_row = jnp.dot(one_hot, gates, preferred_element_type=F32)

    def both_sides(row):
        if sides != 2:
            return lax.all_gather(row, "heads", axis=1, tiled=True)
        other = lax.ppermute(row, "heads", swap)
        return jnp.concatenate([jnp.where(side == 0, row, other), jnp.where(side == 0, other, row)], axis=1)

    rows = jnp.concatenate([both_sides(own_row), both_sides(next_row)], axis=0)
    crossing = jnp.where(last, 0.0, rows[1:2])
    gate_rows = jnp.concatenate([rows[:1], crossing], axis=0)

    per_side = count // sides
    flat = ("queue", "heads")

    def summed(k, pieces, low, *done):
        block = look_up(place, block_of[k])
        rows = after(mix, *done) if done else mix
        delta = project(group, core, half, block * columns + core * half + low, rows, pieces, gate_rows)
        if sides != 2:
            return block, delta, None
        pairs = [
            (q * 2 + 1 - block_of[k][q] // per_side, q * 2 + block_of[k][q] // per_side) for q in range(count)
        ]
        return block, delta, lax.ppermute(delta, flat, pairs)

    results, late, picked = [], [], []
    for n in [1, 0][2 - min(k, 2) :] + list(range(2, k)):
        pieces = [out_weight] if n == 0 else gathered[n, 0]
        if n == k - 1:
            for low, high in chunks:
                picked.append(spread(k, low, high, *picked, *[delta for _, delta, _ in results[-1:]]))
        results.append(summed(n, pieces, 0, *picked, *[delta for _, delta, _ in results[-1:]]))
    sums = [other for _, _, other in results if other is not None]
    for n, (low, _) in enumerate(chunks):
        done = [delta for _, delta, _ in results[-1:]] + [delta for _, (_, delta, _) in late]
        late.append((low, summed(k, gathered[k, low], low, *done, *(sums[2:] if n else sums[:2]))))
    if sides != 2:
        results += [result for _, result in late]
        change = jnp.zeros((2 * frames * tokens, count * half), BF16)
        for n, (block, delta, _) in enumerate(results):
            low = late[n - count + 1][0] if n >= count - 1 else 0
            change = lax.dynamic_update_slice_in_dim(change, delta, block * half + low, axis=1)
        early = lax.psum_scatter(change, "heads", scatter_dimension=1, tiled=True)
        late = []
    else:
        early = []
        for b in range(per_side):
            total = 0.0
            for block, delta, other in results:
                change = delta.astype(F32) + other.astype(F32)
                total = total + jnp.where(block == side * per_side + b, change, 0.0)
            early.append(total)
        early = jnp.concatenate(early, axis=1).astype(BF16)

    mine = frames * tokens
    early_back = lax.ppermute(early[mine:], "seq", swap)
    tail = []
    for low, (block, delta, other) in late:
        total = (delta.astype(F32) + other.astype(F32)).astype(BF16)
        tail.append((low, low + delta.shape[1], block, total[:mine], lax.ppermute(total[mine:], "seq", swap)))

    parts = []
    for b in range(per_side):
        for who in range(2):
            for low, high in chunks:
                at = b * half + low
                change = jnp.where(core == who, early[:mine, at : at + high - low], early_back[:, at : at + high - low])
                change = change.astype(F32)
                for start, _, block, own, back in tail:
                    if start == low:
                        last_part = jnp.where(core == who, own, back).astype(F32)
                        change = change + jnp.where(block == side * per_side + b, last_part, 0.0)
                at = b * columns + who * half + low
                parts.append((moved[:, at : at + high - low].astype(F32) + change).astype(BF16))
    return jnp.concatenate(parts, axis=1).reshape(frames, tokens, features)


def solution(mesh):
    return jax.shard_map(
        local,
        mesh=mesh,
        in_specs=(
            P(("groups", "queue", "seq"), None, "heads"),
            P(None, ("groups", "queue", "seq"), None, "heads"),
            P(("groups", "queue", "seq")),
            P(("groups", "queue")),
            P(None, "heads"),
            P("heads", "queue"),
            P("groups", None, "heads"),
            P("groups", None, None, "heads"),
            P("groups"),
        ),
        out_specs=P(("groups", "queue", "seq"), None, "heads"),
        check_vma=False,
    )
```
